128 devices in a mesh: seq: 64 (over y, x, z_lo, core), head: 2 (over z_hi).
Axes of the slice: x: 4, y: 4, z: 4 (z_hi: 2, z_lo: 2; z = z_hi * 2 + z_lo), core: 2. Of those that a mesh axis runs over, the one named last changes fastest.
Arguments:
- queries: bfloat16 [16384, 2048], P(('seq', 'head')), may hold values from -160 to 160
- key_rows: bfloat16 [16384, 2048], P(('seq', 'head')), may hold values from -4 to 4
- value_rows: bfloat16 [16384, 2048], P(('seq', 'head')), may hold values from -6 to 6
- grad_out: bfloat16 [16384, 2048], P(('seq', 'head')), may hold values from -6 to 6
- anchor: int32 [1], replicated, may hold values from 0 to 31
- offsets: int32 [64], replicated, may hold values from 0 to 256
Outputs:
- attended: bfloat16 [16384, 2048], P(('seq', 'head'))
- grad_queries: bfloat16 [16384, 2048], P(('seq', 'head'))
- grad_keys: bfloat16 [16384, 2048], P(('seq', 'head'))
- grad_values: bfloat16 [16384, 2048], P(('seq', 'head'))
The draws below stay inside these ranges and needn't reach their ends.
All inputs are finite; a program needn't handle non-finite values.
Results may differ from the reference program's by a relative error of at most 0.017.
Values may be sent and summed in bfloat16 or wider, within the bound.
A program may use at most 64 MiB of HBM per device.

```python
import jax
import jax.numpy as jnp
from jax import lax

H = 16
DH = 128
D = 2048
BLOCK = 256
TOKENS = 16384
N_SEQ = 64


def shared_keys(key):
    return jnp.clip(jax.random.normal(key, (TOKENS, D), jnp.float32), -4.0, 4.0)


def draw_key_rows(key, part):
    base_keys = shared_keys(key)
    return base_keys.astype(jnp.bfloat16)


def draw_queries(key, part):
    key = jax.random.fold_in(key, 2)
    drawn = jnp.clip(jax.random.normal(key, (TOKENS, D), jnp.float32), -6.0, 6.0)
    return drawn.astype(jnp.bfloat16)


def touch_ends(drawn, key, smallest, high):
    longest = drawn.shape.index(max(drawn.shape))
    spots = []
    for shift in (0, 1):
        where = [jax.random.randint(jax.random.fold_in(key, axis), (), 0, length) for axis, length in enumerate(drawn.shape)]
        where[longest] = (where[longest] + shift) % drawn.shape[longest]
        spots.append(tuple(where))
    return drawn.at[spots[0]].set(smallest).at[spots[1]].set(high)


def level_of(stream_key, extent, shards, least, top_value):
    level = 1.0
    for dim, shards_of in shards:
        draws = jax.random.uniform(jax.random.fold_in(jax.random.fold_in(stream_key, 6), dim), (shards_of,), jnp.float32, least / len(shards), top_value / len(shards))
        level = level * jnp.repeat(jnp.exp(draws), extent[dim] // shards_of).reshape((-1,) + (1,) * (len(extent) - 1 - dim))
    return level


def noise(stream_key, extent, scale, most, pieces=(), kind=jnp.bfloat16):
    values = scale * jax.random.normal(stream_key, extent, jnp.float32)
    if pieces:
        values = values * level_of(stream_key, extent, pieces, -0.22, 0.18)
    return jnp.clip(values, -most, most).astype(kind)


def setup_inputs(seed: int = 0) -> dict:
    keys = jax.random.split(jax.random.key(seed), 7)
    queries = draw_queries(jax.random.fold_in(keys[6], 71), 0)
    key_rows = draw_key_rows(jax.random.fold_in(keys[6], 71), 0)
    value_rows = noise(keys[2], (TOKENS, D), 1.0, 6.0, ((0, 128),))
    grad_out = noise(keys[3], (TOKENS, D), 1.0, 6.0, ((0, 128),))
    anchor = jax.random.randint(keys[4], (1,), 0, N_SEQ // 2).astype(jnp.int32)
    offsets = touch_ends(jax.random.randint(keys[5], (N_SEQ,), 0, BLOCK + 1), jax.random.fold_in(keys[5], 1), 0, BLOCK).astype(jnp.int32)
    return dict(queries=queries, key_rows=key_rows, value_rows=value_rows, grad_out=grad_out, anchor=anchor, offsets=offsets)


def head_scores(query_rows, keys_own, keys_far, visible):
    score_scale = DH ** -0.5
    length = query_rows.shape[0]
    query_index = lax.broadcasted_iota(jnp.int32, (length, length), 0)
    key_index = lax.broadcasted_iota(jnp.int32, (length, length), 1)
    score_own = jnp.dot(query_rows, keys_own.T, preferred_element_type=jnp.float32) * score_scale
    score_own = jnp.where(query_index >= key_index, score_own, -jnp.inf)
    score_far = jnp.dot(query_rows, keys_far.T, preferred_element_type=jnp.float32) * score_scale
    score_far = jnp.where(visible[None, :], score_far, -jnp.inf)
    return score_own, score_far


def probabilities(score_own, score_far):
    row_max = jnp.maximum(jnp.max(score_own, 1), jnp.max(score_far, 1))
    p_own = jnp.exp(score_own - row_max[:, None])
    p_far = jnp.exp(score_far - row_max[:, None])
    row_total = jnp.sum(p_own, 1) + jnp.sum(p_far, 1)
    return p_own / row_total[:, None], p_far / row_total[:, None]


def forward_head(query_rows, keys_own, values_own, keys_far, values_far, visible):
    score_own, score_far = head_scores(query_rows, keys_own, keys_far, visible)
    p_own, p_far = probabilities(score_own, score_far)
    w_own = p_own.astype(jnp.bfloat16)
    w_far = p_far.astype(jnp.bfloat16)
    mixed = jnp.dot(w_own, values_own, preferred_element_type=jnp.float32)
    mixed = mixed + jnp.dot(w_far, values_far, preferred_element_type=jnp.float32)
    return mixed.astype(jnp.bfloat16), p_own, p_far


def backward_head(query_rows, keys_own, values_own, keys_far, values_far, grad_rows, result, p_own, p_far):
    score_scale = DH ** -0.5
    w_own = p_own.astype(jnp.bfloat16)
    w_far = p_far.astype(jnp.bfloat16)
    row_delta = jnp.sum(grad_rows.astype(jnp.float32) * result.astype(jnp.float32), 1)
    d_own = (p_own * (jnp.dot(grad_rows, values_own.T, preferred_element_type=jnp.float32) - row_delta[:, None])).astype(jnp.bfloat16)
    d_far = (p_far * (jnp.dot(grad_rows, values_far.T, preferred_element_type=jnp.float32) - row_delta[:, None])).astype(jnp.bfloat16)
    grad_q = jnp.dot(d_own, keys_own, preferred_element_type=jnp.float32)
    grad_q = ((grad_q + jnp.dot(d_far, keys_far, preferred_element_type=jnp.float32)) * score_scale).astype(jnp.bfloat16)
    own_k = jnp.dot(d_own.T, query_rows, preferred_element_type=jnp.float32) * score_scale
    own_v = jnp.dot(w_own.T, grad_rows, preferred_element_type=jnp.float32)
    far_k = jnp.dot(d_far.T, query_rows, preferred_element_type=jnp.float32) * score_scale
    far_v = jnp.dot(w_far.T, grad_rows, preferred_element_type=jnp.float32)
    return grad_q, own_k, own_v, far_k, far_v


def blocks(x):
    return x.reshape(N_SEQ, BLOCK, H, DH).transpose(0, 2, 1, 3)


def tokens(x):
    return x.transpose(0, 2, 1, 3).reshape(TOKENS, D)


def reference(queries, key_rows, value_rows, grad_out, anchor, offsets):
    anchor_at = anchor[0]
    q_blocks = blocks(queries)
    k_blocks = blocks(key_rows)
    v_blocks = blocks(value_rows)
    g_blocks = blocks(grad_out)
    k_far = lax.dynamic_index_in_dim(k_blocks, anchor_at, 0, keepdims=False)
    v_far = lax.dynamic_index_in_dim(v_blocks, anchor_at, 0, keepdims=False)
    key_index = jnp.arange(BLOCK, dtype=jnp.int32)

    def block_step(running, block_item):
        q, k, v, g, visible_len, index = block_item
        visible = (index > anchor_at) & (key_index < visible_len)

        def per_head(head_item):
            qh, kh, vh, gh, kf, vf = head_item
            result, p_own, p_far = forward_head(qh, kh, vh, kf, vf, visible)
            grads = backward_head(qh, kh, vh, kf, vf, gh, result, p_own, p_far)
            return (result,) + grads

        result, grad_q, own_k, own_v, far_k, far_v = lax.map(per_head, (q, k, v, g, k_far, v_far))
        return (running[0] + far_k, running[1] + far_v), (result, grad_q, own_k, own_v)

    empty_sum = jnp.zeros((H, BLOCK, DH), jnp.float32)
    block_ids = jnp.arange(N_SEQ, dtype=jnp.int32)
    (sum_k, sum_v), (result, grad_q, own_k, own_v) = lax.scan(block_step, (empty_sum, empty_sum), (q_blocks, k_blocks, v_blocks, g_blocks, offsets, block_ids))
    anchor_k = sum_k.astype(jnp.bfloat16)
    anchor_v = sum_v.astype(jnp.bfloat16)
    is_owner = (block_ids == anchor_at)[:, None, None, None]
    grad_k = (own_k + jnp.where(is_owner, anchor_k.astype(jnp.float32)[None], 0.0)).astype(jnp.bfloat16)
    grad_v = (own_v + jnp.where(is_owner, anchor_v.astype(jnp.float32)[None], 0.0)).astype(jnp.bfloat16)
    return tokens(result), tokens(grad_q), tokens(grad_k), tokens(grad_v)
```

```python
import jax
import jax.numpy as jnp
from jax import lax
from jax.experimental import pallas as pl
from jax.experimental.pallas import tpu as pltpu
from jax.sharding import PartitionSpec as P

DH = 128
BLOCK = 256
HALF = 128
HEADS = 8
WIDE = HEADS * DH
PLANE = 16
SCALE = DH**-0.5
MESH = pl.DeviceIdType.MESH
LOW = -1e30
EARLY = 4


def dot_t(a, b):
    return lax.dot_general(a, b, (((1,), (1,)), ((), ())), preferred_element_type=jnp.float32)


def t_dot(a, b):
    return lax.dot_general(a, b, (((0,), (0,)), ((), ())), preferred_element_type=jnp.float32)


def dot(a, b):
    return jnp.dot(a, b, preferred_element_type=jnp.float32)


def kernel(
    anchor, offsets, q_in, k_in, v_in, g_in,
    att_out, gq_out, gk_out, gv_out,
    qb, gb, kc, vc, sel, cand, zb, kva, fk, rin, zs, zr, an, ank,
    okf, ovf, pk, pr, att_b, gq_b, gk_b, gv_b,
    in_l, in_s, in_r, pv_s, pv_r, s1_s, s1_r, s2_s, s2_r, s3_s, s3_r,
    r1_s, r1_r, r2_s, r2_r, r3_s, r3_r, pg_s, pg_r, out_l, out_s, out_r,
):
    seq = lax.axis_index("seq")
    t = lax.axis_index("head")
    xy = seq // 4
    zl = lax.rem(seq // 2, 2)
    c = lax.rem(seq, 2)
    other = 1 - c
    z = t * 2 + zl
    low_y = xy < 8

    def at(xy_, z_, c_):
        return (xy_ * 4 + lax.rem(z_, 2) * 2 + c_, z_ // 2)

    sibling = at(xy, z, other)
    partner = at(xy, lax.rem(z + 2, 4), c)

    def plane_dev(j):
        return at(j, z, c)

    def z_dev(z_):
        return at(xy, z_, c)

    def remote(src, dst, ss, rs, dev):
        return pltpu.make_async_remote_copy(
            src_ref=src, dst_ref=dst, send_sem=ss, recv_sem=rs, device_id=dev, device_id_type=MESH
        )

    def head_cols(h):
        return pl.ds(pl.multiple_of(h * DH, DH), DH)

    mine = pl.ds(pl.multiple_of(c * WIDE, WIDE), WIDE)
    theirs = pl.ds(pl.multiple_of(other * WIDE, WIDE), WIDE)
    own_rows = pl.ds(HALF, HALF)
    prev_rows = pl.ds(0, HALF)
    all_rows = pl.ds(0, HALF)

    ins = ((k_in, kc, own_rows), (v_in, vc, own_rows), (q_in, qb, all_rows), (g_in, gb, all_rows))
    local_in = [
        pltpu.make_async_copy(src.at[:, mine], buf.at[c, rows, :], in_l.at[i])
        for i, (src, buf, rows) in enumerate(ins)
    ]
    remote_in = [
        remote(src.at[:, theirs], buf.at[c, rows, :], in_s.at[i], in_r.at[i], sibling)
        for i, (src, buf, rows) in enumerate(ins)
    ]
    for copy in local_in:
        copy.start()

    barrier = pltpu.get_barrier_semaphore()
    pl.semaphore_signal(barrier, inc=1, device_id=sibling, device_id_type=MESH)
    for dz in range(1, 4):
        pl.semaphore_signal(barrier, inc=1, device_id=z_dev(lax.rem(z + dz, 4)), device_id_type=MESH)

    @pl.loop(1, PLANE)
    def _(j):
        pl.semaphore_signal(barrier, inc=1, device_id=plane_dev(lax.rem(xy + j, PLANE)), device_id_type=MESH)

    @pl.when(t == 0)
    def _():
        kc[:, 0:HALF, :] = jnp.zeros((2, HALF, WIDE), jnp.bfloat16)
        vc[:, 0:HALF, :] = jnp.zeros((2, HALF, WIDE), jnp.bfloat16)

    pl.semaphore_wait(barrier, 4 + PLANE - 1)

    for copy in remote_in:
        copy.start()

    a = anchor[0]
    a_core = lax.rem(a, 2)
    a_zl = lax.rem(a // 2, 2)
    a_xy = a // 4

    for i in range(2):
        local_in[i].wait()
        remote_in[i].wait_recv()

    for kv, buf in enumerate((kc, vc)):
        for h in range(HEADS):
            cols = slice(h * DH, (h + 1) * DH)
            sel[kv * HEADS + h] = jnp.where(
                a_core == 0, buf[0, HALF:BLOCK, cols], buf[1, HALF:BLOCK, cols]
            )

    def s1_copy(j):
        return remote(sel.at[j], cand.at[lax.rem(xy, 8)], s1_s.at[j], s1_r.at[lax.rem(xy, 8)], plane_dev(j))

    @pl.when(low_y)
    def _():
        @pl.loop(1, PLANE)
        def _(i):
            s1_copy(lax.rem(xy + i, PLANE)).start()

        cand[lax.rem(xy, 8)] = sel[xy]

    def pv_copy(h, i):
        p, buf = i // 2, (kc, vc)[i % 2]
        cols = head_cols(h)
        return remote(
            buf.at[p, own_rows, cols], buf.at[p, prev_rows, cols], pv_s.at[h, i], pv_r.at[h, i], partner
        )

    def send_first_halves(begin, end):
        @pl.when(t == 0)
        def _():
            @pl.loop(begin, end)
            def _(i):
                h = lax.rem(xy + i, HEADS)
                for k in range(4):
                    pv_copy(h, k).start()

    send_first_halves(0, EARLY)

    @pl.loop(0, 8)
    def _(slot):
        @pl.when(slot != xy)
        def _():
            remote(sel.at[0], cand.at[slot], s1_s.at[0], s1_r.at[slot], sibling).wait_recv()

    zb[z] = cand[a_xy]

    def s2_copy(dz):
        return remote(zb.at[z], zb.at[z], s2_s.at[dz], s2_r.at[z], z_dev(lax.rem(z + dz, 4)))

    for dz in range(1, 4):
        s2_copy(dz).start()
    send_first_halves(EARLY, HEADS)
    for dz in range(1, 4):
        slot = lax.rem(z + dz, 4)
        remote(zb.at[slot], zb.at[slot], s2_s.at[dz], s2_r.at[slot], sibling).wait_recv()
    kva[xy, 0:HALF, :] = zb[a_zl]
    kva[xy, HALF:BLOCK, :] = zb[2 + a_zl]

    def s3_copy(j):
        return remote(kva.at[xy], kva.at[xy], s3_s.at[j], s3_r.at[xy], plane_dev(j))

    @pl.loop(0, PLANE - 1)
    def _(i):
        step = i + 1
        j = lax.rem(xy + PLANE - step // 2 + 8 * lax.rem(step, 2), PLANE)
        s3_copy(j).start()

    for i in range(2, 4):
        local_in[i].wait()
        remote_in[i].wait_recv()

    block0 = seq - c
    row = lax.broadcasted_iota(jnp.int32, (HALF, BLOCK), 0)
    col = lax.broadcasted_iota(jnp.int32, (HALF, BLOCK), 1)
    own_ok = jnp.where(col < HALF, jnp.where(t == 1, 1, 0), jnp.where(row >= col - HALF, 1, 0)) > 0
    own_bias = jnp.where(own_ok, 0.0, LOW)
    own_bias = jnp.concatenate([own_bias, own_bias], 0)
    far_bias = jnp.concatenate(
        [
            jnp.where(col < jnp.where(block0 + p > a, offsets[block0 + p], 0), 0.0, LOW)
            for p in range(2)
        ],
        0,
    )

    def r1_copy(j):
        return remote(fk.at[j], rin.at[xy], r1_s.at[j], r1_r.at[xy], plane_dev(j))

    def pg_copy(h):
        return remote(pk.at[h], pr.at[h], pg_s.at[h], pg_r.at[h], partner)

    @pl.loop(0, HEADS)
    def _(i):
        h = lax.rem(xy + i, HEADS)
        cols = head_cols(h)

        for kv in range(2):
            slot = kv * HEADS + h

            @pl.when(slot != xy)
            def _():
                remote(kva.at[slot], kva.at[slot], s3_s.at[0], s3_r.at[slot], sibling).wait_recv()

        @pl.when(t == 1)
        def _():
            for k in range(4):
                pv_copy(h, k).wait_recv()

        q = [qb[p, :, cols] for p in range(2)]
        g = [gb[p, :, cols] for p in range(2)]
        keys = [kc[p, :, cols] for p in range(2)]
        values = [vc[p, :, cols] for p in range(2)]
        q2 = jnp.concatenate(q, 0)
        g2 = jnp.concatenate(g, 0)
        ka = kva[h]
        va = kva[HEADS + h]
        s_far = dot_t(q2, ka) * SCALE + far_bias
        s_own = jnp.concatenate([dot_t(q[p], keys[p]) for p in range(2)], 0) * SCALE + own_bias
        top = jnp.maximum(jnp.max(s_own, 1, keepdims=True), jnp.max(s_far, 1, keepdims=True))
        e_own = jnp.exp(s_own - top)
        e_far = jnp.exp(s_far - top)
        total = jnp.sum(e_own, 1, keepdims=True) + jnp.sum(e_far, 1, keepdims=True)
        inv = 1.0 / total
        p_own = e_own * inv
        p_far = e_far * inv
        w_own = p_own.astype(jnp.bfloat16)
        w_far = p_far.astype(jnp.bfloat16)
        w_half = [w_own[p * HALF : (p + 1) * HALF] for p in range(2)]
        mixed = dot(w_far, va) + jnp.concatenate([dot(w_half[p], values[p]) for p in range(2)], 0)
        att = mixed.astype(jnp.bfloat16)
        delta = jnp.sum(g2.astype(jnp.float32) * att.astype(jnp.float32), 1, keepdims=True)
        d_far = (p_far * (dot_t(g2, va) - delta)).astype(jnp.bfloat16)
        dp_own = jnp.concatenate([dot_t(g[p], values[p]) for p in range(2)], 0)
        d_own = (p_own * (dp_own - delta)).astype(jnp.bfloat16)
        d_half = [d_own[p * HALF : (p + 1) * HALF] for p in range(2)]
        fk[h] = (t_dot(d_far, q2) * SCALE).astype(jnp.bfloat16)
        fk[HEADS + h] = t_dot(w_far, g2).astype(jnp.bfloat16)
        for kv in range(2):
            j = kv * HEADS + h

            @pl.when(j != xy)
            def _():
                r1_copy(j).start()

        for p in range(2):
            own_k = t_dot(d_half[p], q[p]) * SCALE
            own_v = t_dot(w_half[p], g[p])
            pk[h, 0, p] = own_k[:HALF].astype(jnp.bfloat16)
            pk[h, 1, p] = own_v[:HALF].astype(jnp.bfloat16)
            okf[p, :, cols] = own_k[HALF:]
            ovf[p, :, cols] = own_v[HALF:]

        @pl.when(t == 1)
        def _():
            pg_copy(h).start()

        grad_q = dot(d_far, ka) + jnp.concatenate([dot(d_half[p], keys[p]) for p in range(2)], 0)
        grad_q = (grad_q * SCALE).astype(jnp.bfloat16)
        for p in range(2):
            att_b[p, :, cols] = att[p * HALF : (p + 1) * HALF]
            gq_b[p, :, cols] = grad_q[p * HALF : (p + 1) * HALF]

    outs = ((att_b, att_out), (gq_b, gq_out), (gk_b, gk_out), (gv_b, gv_out))
    local_out = [
        pltpu.make_async_copy(buf.at[c], dst.at[:, mine], out_l.at[i]) for i, (buf, dst) in enumerate(outs)
    ]
    remote_out = [
        remote(buf.at[other], dst.at[:, mine], out_s.at[i], out_r.at[i], sibling)
        for i, (buf, dst) in enumerate(outs)
    ]
    for i in range(2):
        remote_out[i].start()
        local_out[i].start()

    @pl.loop(0, PLANE)
    def _(slot):
        @pl.when(slot != xy)
        def _():
            remote(fk.at[slot], rin.at[slot], r1_s.at[0], r1_r.at[slot], sibling).wait_recv()

    rin[xy] = fk[xy]
    acc = rin[0].astype(jnp.float32)
    for slot in range(1, PLANE):
        acc = acc + rin[slot].astype(jnp.float32)
    zs[0] = acc[:HALF].astype(jnp.bfloat16)
    zs[1] = acc[HALF:].astype(jnp.bfloat16)

    def r2_copy(dz):
        z_ = lax.rem(z + dz, 4)
        return remote(zs.at[z_ // 2], zr.at[z], r2_s.at[dz], r2_r.at[z], z_dev(z_))

    for dz in range(1, 4):
        r2_copy(dz).start()
    zr[z] = zs[t]
    for dz in range(1, 4):
        slot = lax.rem(z + dz, 4)
        remote(zs.at[0], zr.at[slot], r2_s.at[dz], r2_r.at[slot], sibling).wait_recv()
    total = zr[0].astype(jnp.float32)
    for slot in range(1, 4):
        total = total + zr[slot].astype(jnp.float32)
    an[...] = total.astype(jnp.bfloat16)

    def r3_copy(j):
        return remote(an, ank.at[xy], r3_s.at[j], r3_r.at[xy], plane_dev(j))

    @pl.loop(0, 8)
    def _(i):
        j = lax.rem(xy + i, 8)

        @pl.when(j != xy)
        def _():
            r3_copy(j).start()

    @pl.when(t == 0)
    def _():
        @pl.loop(0, HEADS)
        def _(i):
            h = lax.rem(xy + i, HEADS)
            pg_copy(h).wait_recv()
            cols = head_cols(h)
            for p in range(2):
                okf[p, :, cols] += pr[h, 0, p].astype(jnp.float32)
                ovf[p, :, cols] += pr[h, 1, p].astype(jnp.float32)

    @pl.when(low_y)
    def _():
        ank[xy] = an[...]

        @pl.loop(0, PLANE)
        def _(slot):
            @pl.when(slot != xy)
            def _():
                remote(an, ank.at[slot], r3_s.at[0], r3_r.at[slot], sibling).wait_recv()

    for p in (other, c):
        for kv, (grads, out) in enumerate(((okf, gk_b), (ovf, gv_b))):
            owner = block0 + p == a

            @pl.when(low_y)
            def _():
                for h in range(HEADS):
                    cols = slice(h * DH, (h + 1) * DH)
                    far = jnp.where(owner, ank[kv * HEADS + h].astype(jnp.float32), 0.0)
                    out[p, :, cols] = (grads[p, :, cols] + far).astype(jnp.bfloat16)

            @pl.when(jnp.logical_not(low_y))
            def _():
                out[p] = grads[p].astype(jnp.bfloat16)

            if p is other:
                remote_out[2 + kv].start()
            else:
                local_out[2 + kv].start()

    for copy in remote_in:
        copy.wait_send()

    @pl.when(low_y)
    def _():
        @pl.loop(1, PLANE)
        def _(i):
            s1_copy(lax.rem(xy + i, PLANE)).wait_send()

    @pl.when(t == 0)
    def _():
        @pl.loop(0, HEADS)
        def _(h):
            for k in range(4):
                pv_copy(h, k).wait_send()

    @pl.when(t == 1)
    def _():
        @pl.loop(0, HEADS)
        def _(h):
            pg_copy(h).wait_send()

    for dz in range(1, 4):
        s2_copy(dz).wait_send()
        r2_copy(dz).wait_send()

    @pl.loop(0, PLANE)
    def _(j):
        @pl.when(j != xy)
        def _():
            s3_copy(j).wait_send()
            r1_copy(j).wait_send()

    @pl.loop(0, 8)
    def _(j):
        @pl.when(j != xy)
        def _():
            r3_copy(j).wait_send()

    for copy in local_out:
        copy.wait()
    for copy in remote_out:
        copy.wait()


def write_out(*refs):
    sems, sems2, hold = refs[8:]
    first = [pltpu.make_async_copy(refs[i], hold.at[i], sems.at[i]) for i in range(4)]
    second = [pltpu.make_async_copy(hold.at[i], refs[4 + i], sems2.at[i]) for i in range(4)]
    for copy in first:
        copy.start()
    for i in range(4):
        first[i].wait()
        second[i].start()
    for copy in second:
        copy.wait()


def on_device(queries, key_rows, value_rows, grad_out, anchor, offsets):
    bf16, f32 = jnp.bfloat16, jnp.float32
    any_spec = pl.BlockSpec(memory_space=pl.ANY)
    smem_spec = pl.BlockSpec(memory_space=pltpu.SMEM)
    dma = pltpu.SemaphoreType.DMA
    half = (HALF, DH)
    whole = (BLOCK, DH)
    scratch = [
        pltpu.VMEM((2, HALF, WIDE), bf16),
        pltpu.VMEM((2, HALF, WIDE), bf16),
        pltpu.VMEM((2, BLOCK, WIDE), bf16),
        pltpu.VMEM((2, BLOCK, WIDE), bf16),
        pltpu.VMEM((PLANE, *half), bf16),
        pltpu.VMEM((8, *half), bf16),
        pltpu.VMEM((4, *half), bf16),
        pltpu.VMEM((PLANE, *whole), bf16),
        pltpu.VMEM((PLANE, *whole), bf16),
        pltpu.VMEM((PLANE, *whole), bf16),
        pltpu.VMEM((2, *half), bf16),
        pltpu.VMEM((4, *half), bf16),
        pltpu.VMEM(half, bf16),
        pltpu.VMEM((PLANE, *half), bf16),
        pltpu.VMEM((2, HALF, WIDE), f32),
        pltpu.VMEM((2, HALF, WIDE), f32),
        pltpu.VMEM((HEADS, 2, 2, *half), bf16),
        pltpu.VMEM((HEADS, 2, 2, *half), bf16),
        pltpu.VMEM((2, HALF, WIDE), bf16),
        pltpu.VMEM((2, HALF, WIDE), bf16),
        pltpu.VMEM((2, HALF, WIDE), bf16),
        pltpu.VMEM((2, HALF, WIDE), bf16),
        dma((4,)), dma((4,)), dma((4,)),
        dma((HEADS, 4)), dma((HEADS, 4)),
        dma((PLANE,)), dma((8,)),
        dma((4,)), dma((4,)),
        dma((PLANE,)), dma((PLANE,)),
        dma((PLANE,)), dma((PLANE,)),
        dma((4,)), dma((4,)),
        dma((8,)), dma((PLANE,)),
        dma((HEADS,)), dma((HEADS,)),
        dma((4,)), dma((4,)), dma((4,)),
    ]
    results = pl.pallas_call(
        kernel,
        out_shape=[jax.ShapeDtypeStruct(queries.shape, bf16)] * 4,
        in_specs=[smem_spec, smem_spec] + [pl.BlockSpec(memory_space=pltpu.HBM)] * 4,
        out_specs=[any_spec] * 4,
        scratch_shapes=scratch,
        compiler_params=pltpu.CompilerParams(
            collective_id=0, has_side_effects=True, vmem_limit_bytes=60 * 2**20
        ),
        name="anchor_attention",
    )(anchor, offsets, queries, key_rows, value_rows, grad_out)
    return pl.pallas_call(
        write_out,
        out_shape=[jax.ShapeDtypeStruct(queries.shape, bf16)] * 4,
        in_specs=[any_spec] * 4,
        out_specs=[pl.BlockSpec(memory_space=pltpu.HBM)] * 4,
        scratch_shapes=[dma((4,)), dma((4,)), pltpu.VMEM((4, *queries.shape), bf16)],
        name="write_out",
    )(*results)


def solution(mesh):
    tokens = P(("seq", "head"), None)
    return jax.shard_map(
        on_device,
        mesh=mesh,
        in_specs=(tokens, tokens, tokens, tokens, P(), P()),
        out_specs=(tokens, tokens, tokens, tokens),
        check_vma=False,
    )
```

```python
import jax
import jax.numpy as jnp
from jax import lax
from jax.experimental import pallas as pl
from jax.experimental.pallas import tpu as pltpu
from jax.sharding import PartitionSpec as P

DH = 128
BLOCK = 256
HALF = 128
HEADS = 8
WIDE = HEADS * DH
PLANE = 16
SCALE = DH**-0.5
MESH = pl.DeviceIdType.MESH
LOW = -1e30
EARLY = 3
EARLY_BACK = 3


def dot_t(a, b):
    return lax.dot_general(a, b, (((1,), (1,)), ((), ())), preferred_element_type=jnp.float32)


def t_dot(a, b):
    return lax.dot_general(a, b, (((0,), (0,)), ((), ())), preferred_element_type=jnp.float32)


def dot(a, b):
    return jnp.dot(a, b, preferred_element_type=jnp.float32)


def kernel(
    anchor, offsets, q_in, k_in, v_in, g_in,
    att_out, gq_out, gk_out, gv_out,
    qb, gb, kc, vc, sel, cand, zb, kva, fk, rin, zs, zr, an, ank,
    okf, ovf, q1b, g1b, st, sr, att_b, gq_b, gk_b, gv_b,
    in_l, in_s, in_r, sw_s, sw_r, s1_s, s1_r, s2_s, s2_r, s3_s, s3_r,
    r1_s, r1_r, r2_s, r2_r, r3_s, r3_r, st_s, st_r, out_l, out_s, out_r,
):
    seq = lax.axis_index("seq")
    t = lax.axis_index("head")
    xy = seq // 4
    zl = lax.rem(seq // 2, 2)
    c = lax.rem(seq, 2)
    other = 1 - c
    z = t * 2 + zl
    low_y = xy < 8

    def at(xy_, z_, c_):
        return (xy_ * 4 + lax.rem(z_, 2) * 2 + c_, z_ // 2)

    sibling = at(xy, z, other)
    partner = at(xy, lax.rem(z + 2, 4), c)

    def plane_dev(j):
        return at(j, z, c)

    def z_dev(z_):
        return at(xy, z_, c)

    def remote(src, dst, ss, rs, dev):
        return pltpu.make_async_remote_copy(
            src_ref=src, dst_ref=dst, send_sem=ss, recv_sem=rs, device_id=dev, device_id_type=MESH
        )

    def head_cols(h):
        return pl.ds(pl.multiple_of(h * DH, DH), DH)

    mine = pl.ds(pl.multiple_of(c * WIDE, WIDE), WIDE)
    theirs = pl.ds(pl.multiple_of(other * WIDE, WIDE), WIDE)
    own_rows = pl.ds(HALF, HALF)
    prev_rows = pl.ds(0, HALF)
    all_rows = pl.ds(0, HALF)

    ins = ((k_in, kc, own_rows), (v_in, vc, own_rows), (q_in, qb, all_rows), (g_in, gb, all_rows))
    local_in = [
        pltpu.make_async_copy(src.at[:, mine], buf.at[c, rows, :], in_l.at[i])
        for i, (src, buf, rows) in enumerate(ins)
    ]
    remote_in = [
        remote(src.at[:, theirs], buf.at[c, rows, :], in_s.at[i], in_r.at[i], sibling)
        for i, (src, buf, rows) in enumerate(ins)
    ]
    for copy in local_in:
        copy.start()

    barrier = pltpu.get_barrier_semaphore()
    pl.semaphore_signal(barrier, inc=1, device_id=sibling, device_id_type=MESH)
    for dz in range(1, 4):
        pl.semaphore_signal(barrier, inc=1, device_id=z_dev(lax.rem(z + dz, 4)), device_id_type=MESH)

    @pl.loop(1, PLANE)
    def _(j):
        pl.semaphore_signal(barrier, inc=1, device_id=plane_dev(lax.rem(xy + j, PLANE)), device_id_type=MESH)

    @pl.when(t == 0)
    def _():
        kc[:, 0:HALF, :] = jnp.zeros((2, HALF, WIDE), jnp.bfloat16)
        vc[:, 0:HALF, :] = jnp.zeros((2, HALF, WIDE), jnp.bfloat16)

    st[...] = jnp.zeros_like(st)
    pl.semaphore_wait(barrier, 4 + PLANE - 1)

    for copy in remote_in:
        copy.start()

    a = anchor[0]
    a_core = lax.rem(a, 2)
    a_zl = lax.rem(a // 2, 2)
    a_xy = a // 4

    for i in range(2):
        local_in[i].wait()
        remote_in[i].wait_recv()

    for kv, buf in enumerate((kc, vc)):
        for h in range(HEADS):
            cols = slice(h * DH, (h + 1) * DH)
            sel[kv * HEADS + h] = jnp.where(
                a_core == 0, buf[0, HALF:BLOCK, cols], buf[1, HALF:BLOCK, cols]
            )

    def s1_copy(j):
        return remote(sel.at[j], cand.at[lax.rem(xy, 8)], s1_s.at[j], s1_r.at[lax.rem(xy, 8)], plane_dev(j))

    @pl.when(low_y)
    def _():
        @pl.loop(1, PLANE)
        def _(i):
            s1_copy(lax.rem(xy + i, PLANE)).start()

        cand[lax.rem(xy, 8)] = sel[xy]

    def swap_copy(h, i, back):
        p = i // 2
        cols = head_cols(h)
        if back:
            buf, far_buf, rows, far_rows = (qb, gb)[i % 2], (q1b, g1b)[i % 2], all_rows, all_rows
        else:
            buf, far_buf, rows, far_rows = (kc, vc)[i % 2], (kc, vc)[i % 2], own_rows, prev_rows
        return remote(
            buf.at[p, rows, cols], far_buf.at[p, far_rows, cols], sw_s.at[h, i], sw_r.at[h, i], partner
        )

    def swap(begin, end, back):
        @pl.when(t == (1 if back else 0))
        def _():
            @pl.loop(begin, end)
            def _(i):
                h = lax.rem(xy + i, HEADS)
                for k in range(4):
                    swap_copy(h, k, back).start()

    swap(0, EARLY, False)
    for i in range(2, 4):
        local_in[i].wait()
        remote_in[i].wait_recv()
    swap(0, EARLY_BACK, True)

    @pl.loop(0, 8)
    def _(slot):
        @pl.when(slot != xy)
        def _():
            remote(sel.at[0], cand.at[slot], s1_s.at[0], s1_r.at[slot], sibling).wait_recv()

    zb[z] = cand[a_xy]

    def s2_copy(dz):
        return remote(zb.at[z], zb.at[z], s2_s.at[dz], s2_r.at[z], z_dev(lax.rem(z + dz, 4)))

    for dz in range(1, 4):
        s2_copy(dz).start()
    for dz in range(1, 4):
        slot = lax.rem(z + dz, 4)
        remote(zb.at[slot], zb.at[slot], s2_s.at[dz], s2_r.at[slot], sibling).wait_recv()
    kva[xy, 0:HALF, :] = zb[a_zl]
    kva[xy, HALF:BLOCK, :] = zb[2 + a_zl]

    def s3_copy(j):
        return remote(kva.at[xy], kva.at[xy], s3_s.at[j], s3_r.at[xy], plane_dev(j))

    @pl.loop(0, PLANE - 1)
    def _(i):
        step = i + 1
        j = lax.rem(xy + PLANE - step // 2 + 8 * lax.rem(step, 2), PLANE)
        s3_copy(j).start()

    block0 = seq - c
    row = lax.broadcasted_iota(jnp.int32, (HALF, BLOCK), 0)
    col = lax.broadcasted_iota(jnp.int32, (HALF, BLOCK), 1)
    own_ok = jnp.where(col < HALF, jnp.where(t == 1, 1, 0), jnp.where(row >= col - HALF, 1, 0)) > 0
    own_bias = jnp.where(own_ok, 0.0, LOW)
    own_bias = jnp.concatenate([own_bias, own_bias], 0)
    far_bias = jnp.concatenate(
        [
            jnp.where(col < jnp.where(block0 + p > a, offsets[block0 + p], 0), 0.0, LOW)
            for p in range(2)
        ],
        0,
    )

    def r1_copy(j):
        return remote(fk.at[j], rin.at[xy], r1_s.at[j], r1_r.at[xy], plane_dev(j))

    def st_copy(b):
        return remote(st.at[b], sr.at[b], st_s.at[b], st_r.at[b], partner)

    lane = lax.broadcasted_iota(jnp.int32, (BLOCK, DH), 1)

    @pl.loop(0, HEADS)
    def _(i):
        h = lax.rem(xy + i, HEADS)
        cols = head_cols(h)

        @pl.when(i < HEADS - EARLY)
        def _():
            swap(i + EARLY, i + EARLY + 1, False)

        @pl.when(i < HEADS - EARLY_BACK)
        def _():
            swap(i + EARLY_BACK, i + EARLY_BACK + 1, True)

        for kv in range(2):
            slot = kv * HEADS + h

            @pl.when(slot != xy)
            def _():
                remote(kva.at[slot], kva.at[slot], s3_s.at[0], s3_r.at[slot], sibling).wait_recv()

        @pl.when(t == 1)
        def _():
            for k in range(4):
                swap_copy(h, k, False).wait_recv()

        q = [qb[p, :, cols] for p in range(2)]
        g = [gb[p, :, cols] for p in range(2)]
        keys = [kc[p, :, cols] for p in range(2)]
        values = [vc[p, :, cols] for p in range(2)]
        q2 = jnp.concatenate(q, 0)
        g2 = jnp.concatenate(g, 0)
        ka = kva[h]
        va = kva[HEADS + h]
        s_far = dot_t(q2, ka) * SCALE + far_bias
        s_own = jnp.concatenate([dot_t(q[p], keys[p]) for p in range(2)], 0) * SCALE + own_bias
        top = jnp.maximum(jnp.max(s_own, 1, keepdims=True), jnp.max(s_far, 1, keepdims=True))
        e_own = jnp.exp(s_own - top)
        e_far = jnp.exp(s_far - top)
        total = jnp.sum(e_own, 1, keepdims=True) + jnp.sum(e_far, 1, keepdims=True)
        inv = 1.0 / total
        p_own = e_own * inv
        p_far = e_far * inv
        w_own = p_own.astype(jnp.bfloat16)
        w_far = p_far.astype(jnp.bfloat16)
        w_half = [w_own[p * HALF : (p + 1) * HALF] for p in range(2)]
        mixed = dot(w_far, va) + jnp.concatenate([dot(w_half[p], values[p]) for p in range(2)], 0)
        att = mixed.astype(jnp.bfloat16)
        delta = jnp.sum(g2.astype(jnp.float32) * att.astype(jnp.float32), 1, keepdims=True)
        d_far = (p_far * (dot_t(g2, va) - delta)).astype(jnp.bfloat16)
        dp_own = jnp.concatenate([dot_t(g[p], values[p]) for p in range(2)], 0)
        d_own = (p_own * (dp_own - delta)).astype(jnp.bfloat16)
        d_half = [d_own[p * HALF : (p + 1) * HALF] for p in range(2)]
        fk[h] = (t_dot(d_far, q2) * SCALE).astype(jnp.bfloat16)
        fk[HEADS + h] = t_dot(w_far, g2).astype(jnp.bfloat16)
        for kv in range(2):
            j = kv * HEADS + h

            @pl.when(j != xy)
            def _():
                r1_copy(j).start()

        batch = i // 4
        place = lax.rem(i, 4) * 4
        stats = st[batch]
        for k, value in enumerate((top, inv, delta)):
            stats = jnp.where(lane == place + k, value, stats)
        st[batch] = stats

        @pl.when(jnp.logical_and(t == 1, lax.rem(i, 4) == 3))
        def _():
            st_copy(batch).start()

        for p in range(2):
            okf[p, :, cols] = t_dot(d_half[p][:, HALF:], q[p]) * SCALE
            ovf[p, :, cols] = t_dot(w_half[p][:, HALF:], g[p])

        grad_q = dot(d_far, ka) + jnp.concatenate([dot(d_half[p], keys[p]) for p in range(2)], 0)
        grad_q = (grad_q * SCALE).astype(jnp.bfloat16)
        for p in range(2):
            att_b[p, :, cols] = att[p * HALF : (p + 1) * HALF]
            gq_b[p, :, cols] = grad_q[p * HALF : (p + 1) * HALF]

    outs = ((att_b, att_out), (gq_b, gq_out), (gk_b, gk_out), (gv_b, gv_out))
    local_out = [
        pltpu.make_async_copy(buf.at[c], dst.at[:, mine], out_l.at[i]) for i, (buf, dst) in enumerate(outs)
    ]
    remote_out = [
        remote(buf.at[other], dst.at[:, mine], out_s.at[i], out_r.at[i], sibling)
        for i, (buf, dst) in enumerate(outs)
    ]
    for i in range(2):
        remote_out[i].start()
        local_out[i].start()

    def cross(begin, end):
        @pl.when(t == 0)
        def _():
            for b in range(begin // 4, (end + 3) // 4):
                if begin <= 4 * b:
                    st_copy(b).wait_recv()

            @pl.loop(begin, end)
            def _(i):
                h = lax.rem(xy + i, HEADS)
                cols = head_cols(h)
                for k in range(4):
                    swap_copy(h, k, True).wait_recv()
                stats = sr[i // 4]
                place = lax.rem(i, 4) * 4
                top, inv, delta = [
                    jnp.sum(jnp.where(lane == place + k, stats, 0.0), 1, keepdims=True) for k in range(3)
                ]
                q = [q1b[p, :, cols] for p in range(2)]
                g = [g1b[p, :, cols] for p in range(2)]
                s = jnp.concatenate([dot_t(q[p], kc[p, HALF:BLOCK, cols]) for p in range(2)], 0) * SCALE
                dp = jnp.concatenate([dot_t(g[p], vc[p, HALF:BLOCK, cols]) for p in range(2)], 0)
                prob = jnp.exp(s - top) * inv
                w = prob.astype(jnp.bfloat16)
                d = (prob * (dp - delta)).astype(jnp.bfloat16)
                for p in range(2):
                    rows = slice(p * HALF, (p + 1) * HALF)
                    okf[p, :, cols] += t_dot(d[rows], q[p]) * SCALE
                    ovf[p, :, cols] += t_dot(w[rows], g[p])

    cross(0, 4)

    @pl.loop(0, PLANE)
    def _(slot):
        @pl.when(slot != xy)
        def _():
            remote(fk.at[slot], rin.at[slot], r1_s.at[0], r1_r.at[slot], sibling).wait_recv()

    rin[xy] = fk[xy]
    acc = rin[0].astype(jnp.float32)
    for slot in range(1, PLANE):
        acc = acc + rin[slot].astype(jnp.float32)
    zs[0] = acc[:HALF].astype(jnp.bfloat16)
    zs[1] = acc[HALF:].astype(jnp.bfloat16)

    def r2_copy(dz):
        z_ = lax.rem(z + dz, 4)
        return remote(zs.at[z_ // 2], zr.at[z], r2_s.at[dz], r2_r.at[z], z_dev(z_))

    for dz in range(1, 4):
        r2_copy(dz).start()
    zr[z] = zs[t]
    cross(4, 6)
    for dz in range(1, 4):
        slot = lax.rem(z + dz, 4)
        remote(zs.at[0], zr.at[slot], r2_s.at[dz], r2_r.at[slot], sibling).wait_recv()
    total = zr[0].astype(jnp.float32)
    for slot in range(1, 4):
        total = total + zr[slot].astype(jnp.float32)
    an[...] = total.astype(jnp.bfloat16)

    def r3_copy(j):
        return remote(an, ank.at[xy], r3_s.at[j], r3_r.at[xy], plane_dev(j))

    @pl.loop(0, 8)
    def _(i):
        j = lax.rem(xy + i, 8)

        @pl.when(j != xy)
        def _():
            r3_copy(j).start()

    cross(6, HEADS)

    @pl.when(low_y)
    def _():
        ank[xy] = an[...]

        @pl.loop(0, PLANE)
        def _(slot):
            @pl.when(slot != xy)
            def _():
                remote(an, ank.at[slot], r3_s.at[0], r3_r.at[slot], sibling).wait_recv()

    for p in (other, c):
        for kv, (grads, out) in enumerate(((okf, gk_b), (ovf, gv_b))):
            owner = block0 + p == a

            @pl.when(low_y)
            def _():
                for h in range(HEADS):
                    cols = slice(h * DH, (h + 1) * DH)
                    far = jnp.where(owner, ank[kv * HEADS + h].astype(jnp.float32), 0.0)
                    out[p, :, cols] = (grads[p, :, cols] + far).astype(jnp.bfloat16)

            @pl.when(jnp.logical_not(low_y))
            def _():
                out[p] = grads[p].astype(jnp.bfloat16)

            if p is other:
                remote_out[2 + kv].start()
            else:
                local_out[2 + kv].start()

    for copy in remote_in:
        copy.wait_send()

    @pl.when(low_y)
    def _():
        @pl.loop(1, PLANE)
        def _(i):
            s1_copy(lax.rem(xy + i, PLANE)).wait_send()

    for back in (False, True):

        @pl.when(t == (1 if back else 0))
        def _():
            @pl.loop(0, HEADS)
            def _(h):
                for k in range(4):
                    swap_copy(h, k, back).wait_send()

    @pl.when(t == 1)
    def _():
        for b in range(2):
            st_copy(b).wait_send()

    for dz in range(1, 4):
        s2_copy(dz).wait_send()
        r2_copy(dz).wait_send()

    @pl.loop(0, PLANE)
    def _(j):
        @pl.when(j != xy)
        def _():
            s3_copy(j).wait_send()
            r1_copy(j).wait_send()

    @pl.loop(0, 8)
    def _(j):
        @pl.when(j != xy)
        def _():
            r3_copy(j).wait_send()

    for copy in local_out:
        copy.wait()
    for copy in remote_out:
        copy.wait()


def write_out(*refs):
    sems, sems2, hold = refs[8:]
    first = [pltpu.make_async_copy(refs[i], hold.at[i], sems.at[i]) for i in range(4)]
    second = [pltpu.make_async_copy(hold.at[i], refs[4 + i], sems2.at[i]) for i in range(4)]
    for copy in first:
        copy.start()
    for i in range(4):
        first[i].wait()
        second[i].start()
    for copy in second:
        copy.wait()


def on_device(queries, key_rows, value_rows, grad_out, anchor, offsets):
    bf16, f32 = jnp.bfloat16, jnp.float32
    any_spec = pl.BlockSpec(memory_space=pl.ANY)
    smem_spec = pl.BlockSpec(memory_space=pltpu.SMEM)
    dma = pltpu.SemaphoreType.DMA
    half = (HALF, DH)
    whole = (BLOCK, DH)
    scratch = [
        pltpu.VMEM((2, HALF, WIDE), bf16),
        pltpu.VMEM((2, HALF, WIDE), bf16),
        pltpu.VMEM((2, BLOCK, WIDE), bf16),
        pltpu.VMEM((2, BLOCK, WIDE), bf16),
        pltpu.VMEM((PLANE, *half), bf16),
        pltpu.VMEM((8, *half), bf16),
        pltpu.VMEM((4, *half), bf16),
        pltpu.VMEM((PLANE, *whole), bf16),
        pltpu.VMEM((PLANE, *whole), bf16),
        pltpu.VMEM((PLANE, *whole), bf16),
        pltpu.VMEM((2, *half), bf16),
        pltpu.VMEM((4, *half), bf16),
        pltpu.VMEM(half, bf16),
        pltpu.VMEM((PLANE, *half), bf16),
        pltpu.VMEM((2, HALF, WIDE), f32),
        pltpu.VMEM((2, HALF, WIDE), f32),
        pltpu.VMEM((2, HALF, WIDE), bf16),
        pltpu.VMEM((2, HALF, WIDE), bf16),
        pltpu.VMEM((2, BLOCK, DH), f32),
        pltpu.VMEM((2, BLOCK, DH), f32),
        pltpu.VMEM((2, HALF, WIDE), bf16),
        pltpu.VMEM((2, HALF, WIDE), bf16),
        pltpu.VMEM((2, HALF, WIDE), bf16),
        pltpu.VMEM((2, HALF, WIDE), bf16),
        dma((4,)), dma((4,)), dma((4,)),
        dma((HEADS, 4)), dma((HEADS, 4)),
        dma((PLANE,)), dma((8,)),
        dma((4,)), dma((4,)),
        dma((PLANE,)), dma((PLANE,)),
        dma((PLANE,)), dma((PLANE,)),
        dma((4,)), dma((4,)),
        dma((8,)), dma((PLANE,)),
        dma((2,)), dma((2,)),
        dma((4,)), dma((4,)), dma((4,)),
    ]
    results = pl.pallas_call(
        kernel,
        out_shape=[jax.ShapeDtypeStruct(queries.shape, bf16)] * 4,
        in_specs=[smem_spec, smem_spec] + [pl.BlockSpec(memory_space=pltpu.HBM)] * 4,
        out_specs=[any_spec] * 4,
        scratch_shapes=scratch,
        compiler_params=pltpu.CompilerParams(
            collective_id=0, has_side_effects=True, vmem_limit_bytes=60 * 2**20
        ),
        name="anchor_attention",
    )(anchor, offsets, queries, key_rows, value_rows, grad_out)
    return pl.pallas_call(
        write_out,
        out_shape=[jax.ShapeDtypeStruct(queries.shape, bf16)] * 4,
        in_specs=[any_spec] * 4,
        out_specs=[pl.BlockSpec(memory_space=pltpu.HBM)] * 4,
        scratch_shapes=[dma((4,)), dma((4,)), pltpu.VMEM((4, *queries.shape), bf16)],
        name="write_out",
    )(*results)


def solution(mesh):
    tokens = P(("seq", "head"), None)
    return jax.shard_map(
        on_device,
        mesh=mesh,
        in_specs=(tokens, tokens, tokens, tokens, P(), P()),
        out_specs=(tokens, tokens, tokens, tokens),
        check_vma=False,
    )
```

```python
import jax
import jax.numpy as jnp
from jax import lax
from jax.experimental import pallas as pl
from jax.experimental.pallas import tpu as pltpu
from jax.sharding import PartitionSpec as P

DH = 128
BLOCK = 256
HALF = 128
HEADS = 8
WIDE = HEADS * DH
PLANE = 16
SCALE = DH**-0.5
MESH = pl.DeviceIdType.MESH
LOW = -1e30
EARLY = 3
AHEAD = 5


def dot_t(a, b):
    return lax.dot_general(a, b, (((1,), (1,)), ((), ())), preferred_element_type=jnp.float32)


def t_dot(a, b):
    return lax.dot_general(a, b, (((0,), (0,)), ((), ())), preferred_element_type=jnp.float32)


def dot(a, b):
    return jnp.dot(a, b, preferred_element_type=jnp.float32)


def kernel(
    anchor, offsets, q_in, k_in, v_in, g_in,
    att_out, gq_out, gk_out, gv_out,
    qb, gb, kc, vc, sel, cand, zb, kva, fk, rin, zs, zr, an, ank,
    okf, ovf, q1b, g1b, st, sr, att_b, gq_b, gk_b, gv_b,
    in_l, in_s, in_r, sw_s, sw_r, s1_s, s1_r, s2_s, s2_r, s3_s, s3_r,
    r1_s, r1_r, r2_s, r2_r, r3_s, r3_r, st_s, st_r, out_l, out_s, out_r,
):
    seq = lax.axis_index("seq")
    t = lax.axis_index("head")
    xy = seq // 4
    zl = lax.rem(seq // 2, 2)
    c = lax.rem(seq, 2)
    other = 1 - c
    z = t * 2 + zl
    low_y = xy < 8

    def at(xy_, z_, c_):
        return (xy_ * 4 + lax.rem(z_, 2) * 2 + c_, z_ // 2)

    sibling = at(xy, z, other)
    partner = at(xy, lax.rem(z + 2, 4), c)

    def plane_dev(j):
        return at(j, z, c)

    def z_dev(z_):
        return at(xy, z_, c)

    def remote(src, dst, ss, rs, dev):
        return pltpu.make_async_remote_copy(
            src_ref=src, dst_ref=dst, send_sem=ss, recv_sem=rs, device_id=dev, device_id_type=MESH
        )

    def sent(shape_of, sem):
        remote(shape_of, shape_of, sem, sem, sibling).wait_send()

    def landed(shape_of, sem):
        remote(shape_of, shape_of, sem, sem, sibling).wait_recv()

    def head_cols(h):
        return pl.ds(pl.multiple_of(h * DH, DH), DH)

    mine = pl.ds(pl.multiple_of(c * WIDE, WIDE), WIDE)
    theirs = pl.ds(pl.multiple_of(other * WIDE, WIDE), WIDE)
    own_rows = pl.ds(HALF, HALF)
    prev_rows = pl.ds(0, HALF)
    all_rows = pl.ds(0, HALF)

    ins = ((k_in, kc, own_rows), (v_in, vc, own_rows), (q_in, qb, all_rows), (g_in, gb, all_rows))
    local_in = [
        pltpu.make_async_copy(src.at[:, mine], buf.at[c, rows, :], in_l.at[i])
        for i, (src, buf, rows) in enumerate(ins)
    ]
    remote_in = [
        remote(src.at[:, theirs], buf.at[c, rows, :], in_s.at[i], in_r.at[i], sibling)
        for i, (src, buf, rows) in enumerate(ins)
    ]
    for copy in local_in:
        copy.start()

    barrier = pltpu.get_barrier_semaphore()
    pl.semaphore_signal(barrier, inc=1, device_id=sibling, device_id_type=MESH)
    for dz in range(1, 4):
        pl.semaphore_signal(barrier, inc=1, device_id=z_dev(lax.rem(z + dz, 4)), device_id_type=MESH)

    @pl.loop(1, PLANE)
    def _(j):
        pl.semaphore_signal(barrier, inc=1, device_id=plane_dev(lax.rem(xy + j, PLANE)), device_id_type=MESH)

    @pl.when(t == 0)
    def _():
        kc[:, 0:HALF, :] = jnp.zeros((2, HALF, WIDE), jnp.bfloat16)
        vc[:, 0:HALF, :] = jnp.zeros((2, HALF, WIDE), jnp.bfloat16)

    st[...] = jnp.zeros_like(st)
    pl.semaphore_wait(barrier, 4 + PLANE - 1)

    for copy in remote_in:
        copy.start()

    a = anchor[0]
    a_core = lax.rem(a, 2)
    a_zl = lax.rem(a // 2, 2)
    a_xy = a // 4

    for i in range(2):
        local_in[i].wait()
        remote_in[i].wait_recv()

    for kv, buf in enumerate((kc, vc)):
        for h in range(HEADS):
            cols = slice(h * DH, (h + 1) * DH)
            sel[kv * HEADS + h] = jnp.where(
                a_core == 0, buf[0, HALF:BLOCK, cols], buf[1, HALF:BLOCK, cols]
            )

    def s1_copy(j):
        return remote(sel.at[j], cand.at[lax.rem(xy, 8)], s1_s, s1_r, plane_dev(j))

    @pl.when(low_y)
    def _():
        @pl.loop(1, PLANE)
        def _(i):
            s1_copy(lax.rem(xy + i, PLANE)).start()

        cand[lax.rem(xy, 8)] = sel[xy]

    def swap_copy(h, i, back):
        p = i // 2
        cols = head_cols(h)
        if back:
            buf, far_buf, rows, far_rows = (qb, gb)[i % 2], (q1b, g1b)[i % 2], all_rows, all_rows
        else:
            buf, far_buf, rows, far_rows = (kc, vc)[i % 2], (kc, vc)[i % 2], own_rows, prev_rows
        return remote(
            buf.at[p, rows, cols], far_buf.at[p, far_rows, cols], sw_s, sw_r.at[h], partner
        )

    def swap(begin, end, back):
        @pl.when(t == (1 if back else 0))
        def _():
            @pl.loop(begin, end)
            def _(i):
                h = lax.rem(xy + i, HEADS)
                for k in range(4):
                    swap_copy(h, k, back).start()

    swap(0, EARLY, False)
    for i in range(2, 4):
        local_in[i].wait()
        remote_in[i].wait_recv()
    swap(0, EARLY, True)

    @pl.when(low_y)
    def _():
        landed(cand.at[pl.ds(0, 7)], s1_r)

    @pl.when(jnp.logical_not(low_y))
    def _():
        landed(cand, s1_r)

    zb[z] = cand[a_xy]

    def s2_copy(dz):
        return remote(zb.at[z], zb.at[z], s2_s, s2_r, z_dev(lax.rem(z + dz, 4)))

    for dz in range(1, 4):
        s2_copy(dz).start()
    landed(zb.at[pl.ds(0, 3)], s2_r)
    kva[xy, 0:HALF, :] = zb[a_zl]
    kva[xy, HALF:BLOCK, :] = zb[2 + a_zl]

    def s3_copy(j):
        return remote(kva.at[xy], kva.at[xy], s3_s, s3_r.at[xy], plane_dev(j))

    @pl.loop(0, PLANE - 1)
    def _(i):
        step = i + 1
        j = lax.rem(xy + PLANE - step // 2 + 8 * lax.rem(step, 2), PLANE)
        s3_copy(j).start()

    swap(EARLY, AHEAD, False)
    swap(EARLY, AHEAD, True)
    block0 = seq - c
    row = lax.broadcasted_iota(jnp.int32, (HALF, BLOCK), 0)
    col = lax.broadcasted_iota(jnp.int32, (HALF, BLOCK), 1)
    own_ok = jnp.where(col < HALF, jnp.where(t == 1, 1, 0), jnp.where(row >= col - HALF, 1, 0)) > 0
    own_bias = jnp.where(own_ok, 0.0, LOW)
    own_bias = jnp.concatenate([own_bias, own_bias], 0)
    far_bias = jnp.concatenate(
        [
            jnp.where(col < jnp.where(block0 + p > a, offsets[block0 + p], 0), 0.0, LOW)
            for p in range(2)
        ],
        0,
    )

    def r1_copy(j):
        return remote(fk.at[j], rin.at[xy], r1_s, r1_r, plane_dev(j))

    def st_copy(b):
        return remote(st.at[b], sr.at[b], st_s.at[b], st_r.at[b], partner)

    lane = lax.broadcasted_iota(jnp.int32, (BLOCK, DH), 1)

    @pl.loop(0, HEADS)
    def _(i):
        h = lax.rem(xy + i, HEADS)
        cols = head_cols(h)

        @pl.when(i < HEADS - AHEAD)
        def _():
            swap(i + AHEAD, i + AHEAD + 1, False)
            swap(i + AHEAD, i + AHEAD + 1, True)

        for kv in range(2):
            slot = kv * HEADS + h

            @pl.when(slot != xy)
            def _():
                landed(kva.at[slot], s3_r.at[slot])

        @pl.when(t == 1)
        def _():
            landed(cand.at[pl.ds(0, 4)], sw_r.at[h])

        q = [qb[p, :, cols] for p in range(2)]
        g = [gb[p, :, cols] for p in range(2)]
        keys = [kc[p, :, cols] for p in range(2)]
        values = [vc[p, :, cols] for p in range(2)]
        q2 = jnp.concatenate(q, 0)
        g2 = jnp.concatenate(g, 0)
        ka = kva[h]
        va = kva[HEADS + h]
        s_far = dot_t(q2, ka) * SCALE + far_bias
        s_own = jnp.concatenate([dot_t(q[p], keys[p]) for p in range(2)], 0) * SCALE + own_bias
        top = jnp.maximum(jnp.max(s_own, 1, keepdims=True), jnp.max(s_far, 1, keepdims=True))
        e_own = jnp.exp(s_own - top)
        e_far = jnp.exp(s_far - top)
        total = jnp.sum(e_own, 1, keepdims=True) + jnp.sum(e_far, 1, keepdims=True)
        inv = 1.0 / total
        p_own = e_own * inv
        p_far = e_far * inv
        w_own = p_own.astype(jnp.bfloat16)
        w_far = p_far.astype(jnp.bfloat16)
        w_half = [w_own[p * HALF : (p + 1) * HALF] for p in range(2)]
        mixed = dot(w_far, va) + jnp.concatenate([dot(w_half[p], values[p]) for p in range(2)], 0)
        att = mixed.astype(jnp.bfloat16)
        delta = jnp.sum(g2.astype(jnp.float32) * att.astype(jnp.float32), 1, keepdims=True)
        d_far = (p_far * (dot_t(g2, va) - delta)).astype(jnp.bfloat16)
        dp_own = jnp.concatenate([dot_t(g[p], values[p]) for p in range(2)], 0)
        d_own = (p_own * (dp_own - delta)).astype(jnp.bfloat16)
        d_half = [d_own[p * HALF : (p + 1) * HALF] for p in range(2)]
        fk[h] = (t_dot(d_far, q2) * SCALE).astype(jnp.bfloat16)
        fk[HEADS + h] = t_dot(w_far, g2).astype(jnp.bfloat16)
        for kv in range(2):
            j = kv * HEADS + h

            @pl.when(j != xy)
            def _():
                r1_copy(j).start()

        batch = i // 4
        place = lax.rem(i, 4) * 4
        stats = st[batch]
        for k, value in enumerate((top, inv, delta)):
            stats = jnp.where(lane == place + k, value, stats)
        st[batch] = stats

        @pl.when(jnp.logical_and(t == 1, lax.rem(i, 4) == 3))
        def _():
            st_copy(batch).start()

        for p in range(2):
            okf[p, :, cols] = t_dot(d_half[p][:, HALF:], q[p]) * SCALE
            ovf[p, :, cols] = t_dot(w_half[p][:, HALF:], g[p])

        grad_q = dot(d_far, ka) + jnp.concatenate([dot(d_half[p], keys[p]) for p in range(2)], 0)
        grad_q = (grad_q * SCALE).astype(jnp.bfloat16)
        for p in range(2):
            att_b[p, :, cols] = att[p * HALF : (p + 1) * HALF]
            gq_b[p, :, cols] = grad_q[p * HALF : (p + 1) * HALF]

    outs = ((att_b, att_out), (gq_b, gq_out), (gk_b, gk_out), (gv_b, gv_out))
    local_out = [
        pltpu.make_async_copy(buf.at[c], dst.at[:, mine], out_l.at[i]) for i, (buf, dst) in enumerate(outs)
    ]
    remote_out = [
        remote(buf.at[other], dst.at[:, mine], out_s.at[i], out_r.at[i], sibling)
        for i, (buf, dst) in enumerate(outs)
    ]
    for i in range(2):
        remote_out[i].start()
        local_out[i].start()

    def cross(begin, end):
        @pl.when(t == 0)
        def _():
            for b in range(begin // 4, (end + 3) // 4):
                if begin <= 4 * b:
                    st_copy(b).wait_recv()

            @pl.loop(begin, end)
            def _(i):
                h = lax.rem(xy + i, HEADS)
                cols = head_cols(h)
                landed(cand.at[pl.ds(0, 4)], sw_r.at[h])
                stats = sr[i // 4]
                place = lax.rem(i, 4) * 4
                top, inv, delta = [
                    jnp.sum(jnp.where(lane == place + k, stats, 0.0), 1, keepdims=True) for k in range(3)
                ]
                q = [q1b[p, :, cols] for p in range(2)]
                g = [g1b[p, :, cols] for p in range(2)]
                s = jnp.concatenate([dot_t(q[p], kc[p, HALF:BLOCK, cols]) for p in range(2)], 0) * SCALE
                dp = jnp.concatenate([dot_t(g[p], vc[p, HALF:BLOCK, cols]) for p in range(2)], 0)
                prob = jnp.exp(s - top) * inv
                w = prob.astype(jnp.bfloat16)
                d = (prob * (dp - delta)).astype(jnp.bfloat16)
                for p in range(2):
                    rows = slice(p * HALF, (p + 1) * HALF)
                    okf[p, :, cols] += t_dot(d[rows], q[p]) * SCALE
                    ovf[p, :, cols] += t_dot(w[rows], g[p])

    for copy in remote_in:
        copy.wait_send()

    @pl.when(low_y)
    def _():
        sent(sel.at[pl.ds(0, PLANE - 1)], s1_s)

    sent(zb.at[pl.ds(0, 3)], s2_s)
    sent(kva.at[pl.ds(0, PLANE - 1)], s3_s)
    sent(kc, sw_s)

    cross(0, 4)

    landed(rin.at[pl.ds(0, PLANE - 1)], r1_r)
    rin[xy] = fk[xy]
    acc = rin[0].astype(jnp.float32)
    for slot in range(1, PLANE):
        acc = acc + rin[slot].astype(jnp.float32)
    zs[0] = acc[:HALF].astype(jnp.bfloat16)
    zs[1] = acc[HALF:].astype(jnp.bfloat16)

    def r2_copy(dz):
        z_ = lax.rem(z + dz, 4)
        return remote(zs.at[z_ // 2], zr.at[z], r2_s, r2_r, z_dev(z_))

    for dz in range(1, 4):
        r2_copy(dz).start()
    zr[z] = zs[t]
    cross(4, 6)
    sent(fk.at[pl.ds(0, PLANE - 1)], r1_s)
    landed(zr.at[pl.ds(0, 3)], r2_r)
    total = zr[0].astype(jnp.float32)
    for slot in range(1, 4):
        total = total + zr[slot].astype(jnp.float32)
    an[...] = total.astype(jnp.bfloat16)

    def r3_copy(j):
        return remote(an, ank.at[xy], r3_s, r3_r, plane_dev(j))

    @pl.loop(0, 8)
    def _(i):
        j = lax.rem(xy + i, 8)

        @pl.when(j != xy)
        def _():
            r3_copy(j).start()

    cross(6, HEADS)
    sent(zr.at[pl.ds(0, 3)], r2_s)

    @pl.when(t == 1)
    def _():
        for b in range(2):
            st_copy(b).wait_send()

    @pl.when(low_y)
    def _():
        ank[xy] = an[...]
        landed(ank.at[pl.ds(0, PLANE - 1)], r3_r)

    for p in (other, c):
        for kv, (grads, out) in enumerate(((okf, gk_b), (ovf, gv_b))):
            owner = block0 + p == a

            @pl.when(low_y)
            def _():
                for h in range(HEADS):
                    cols = slice(h * DH, (h + 1) * DH)
                    far = jnp.where(owner, ank[kv * HEADS + h].astype(jnp.float32), 0.0)
                    out[p, :, cols] = (grads[p, :, cols] + far).astype(jnp.bfloat16)

            @pl.when(jnp.logical_not(low_y))
            def _():
                out[p] = grads[p].astype(jnp.bfloat16)

            if p is other:
                remote_out[2 + kv].start()
            else:
                local_out[2 + kv].start()

    @pl.when(low_y)
    def _():
        sent(ank.at[pl.ds(0, 7)], r3_s)

    @pl.when(jnp.logical_not(low_y))
    def _():
        sent(ank.at[pl.ds(0, 8)], r3_s)

    for copy in local_out:
        copy.wait()
    for copy in remote_out:
        copy.wait()


def write_out(*refs):
    sems, sems2, hold = refs[8:]
    first = [pltpu.make_async_copy(refs[i], hold.at[i], sems.at[i]) for i in range(4)]
    second = [pltpu.make_async_copy(hold.at[i], refs[4 + i], sems2.at[i]) for i in range(4)]
    for copy in first:
        copy.start()
    for i in range(4):
        first[i].wait()
        second[i].start()
    for copy in second:
        copy.wait()


def on_device(queries, key_rows, value_rows, grad_out, anchor, offsets):
    bf16, f32 = jnp.bfloat16, jnp.float32
    any_spec = pl.BlockSpec(memory_space=pl.ANY)
    smem_spec = pl.BlockSpec(memory_space=pltpu.SMEM)
    dma = pltpu.SemaphoreType.DMA
    half = (HALF, DH)
    whole = (BLOCK, DH)
    scratch = [
        pltpu.VMEM((2, HALF, WIDE), bf16),
        pltpu.VMEM((2, HALF, WIDE), bf16),
        pltpu.VMEM((2, BLOCK, WIDE), bf16),
        pltpu.VMEM((2, BLOCK, WIDE), bf16),
        pltpu.VMEM((PLANE, *half), bf16),
        pltpu.VMEM((8, *half), bf16),
        pltpu.VMEM((4, *half), bf16),
        pltpu.VMEM((PLANE, *whole), bf16),
        pltpu.VMEM((PLANE, *whole), bf16),
        pltpu.VMEM((PLANE, *whole), bf16),
        pltpu.VMEM((2, *half), bf16),
        pltpu.VMEM((4, *half), bf16),
        pltpu.VMEM(half, bf16),
        pltpu.VMEM((PLANE, *half), bf16),
        pltpu.VMEM((2, HALF, WIDE), f32),
        pltpu.VMEM((2, HALF, WIDE), f32),
        pltpu.VMEM((2, HALF, WIDE), bf16),
        pltpu.VMEM((2, HALF, WIDE), bf16),
        pltpu.VMEM((2, BLOCK, DH), f32),
        pltpu.VMEM((2, BLOCK, DH), f32),
        pltpu.VMEM((2, HALF, WIDE), bf16),
        pltpu.VMEM((2, HALF, WIDE), bf16),
        pltpu.VMEM((2, HALF, WIDE), bf16),
        pltpu.VMEM((2, HALF, WIDE), bf16),
        dma((4,)), dma((4,)), dma((4,)),
        dma, dma((HEADS,)),
        dma, dma,
        dma, dma,
        dma, dma((PLANE,)),
        dma, dma,
        dma, dma,
        dma, dma,
        dma((2,)), dma((2,)),
        dma((4,)), dma((4,)), dma((4,)),
    ]
    results = pl.pallas_call(
        kernel,
        out_shape=[jax.ShapeDtypeStruct(queries.shape, bf16)] * 4,
        in_specs=[smem_spec, smem_spec] + [pl.BlockSpec(memory_space=pltpu.HBM)] * 4,
        out_specs=[any_spec] * 4,
        scratch_shapes=scratch,
        compiler_params=pltpu.CompilerParams(
            collective_id=0, has_side_effects=True, vmem_limit_bytes=60 * 2**20
        ),
        name="anchor_attention",
    )(anchor, offsets, queries, key_rows, value_rows, grad_out)
    return pl.pallas_call(
        write_out,
        out_shape=[jax.ShapeDtypeStruct(queries.shape, bf16)] * 4,
        in_specs=[any_spec] * 4,
        out_specs=[pl.BlockSpec(memory_space=pltpu.HBM)] * 4,
        scratch_shapes=[dma((4,)), dma((4,)), pltpu.VMEM((4, *queries.shape), bf16)],
        name="write_out",
    )(*results)


def solution(mesh):
    tokens = P(("seq", "head"), None)
    return jax.shard_map(
        on_device,
        mesh=mesh,
        in_specs=(tokens, tokens, tokens, tokens, P(), P()),
        out_specs=(tokens, tokens, tokens, tokens),
        check_vma=False,
    )
```

```python
import jax
import jax.numpy as jnp
from jax import lax
from jax.experimental import pallas as pl
from jax.experimental.pallas import tpu as pltpu
from jax.sharding import PartitionSpec as P

DH = 128
BLOCK = 256
HALF = 128
HEADS = 8
WIDE = HEADS * DH
PLANE = 16
SCALE = DH**-0.5
MESH = pl.DeviceIdType.MESH
LOW = -1e30
EARLY = 4
AHEAD = 5


def dot_t(a, b):
    return lax.dot_general(a, b, (((1,), (1,)), ((), ())), preferred_element_type=jnp.float32)


def t_dot(a, b):
    return lax.dot_general(a, b, (((0,), (0,)), ((), ())), preferred_element_type=jnp.float32)


def dot(a, b):
    return jnp.dot(a, b, preferred_element_type=jnp.float32)


def kernel(
    anchor, offsets, q_in, k_in, v_in, g_in,
    att_out, gq_out, gk_out, gv_out,
    qb, gb, kc, vc, sel, cand, zb, kva, fk, rin, zs, zr, an, ank,
    okf, ovf, q1b, g1b, st, sr, att_b, gq_b, gk_b, gv_b,
    in_l, in_s, in_r, sw_s, sw_r, s1_s, s1_r, s2_s, s2_r, s3_s, s3_r,
    r1_s, r1_r, r2_s, r2_r, r3_s, r3_r, st_s, st_r, out_l, out_s, out_r,
):
    seq = lax.axis_index("seq")
    t = lax.axis_index("head")
    xy = seq // 4
    zl = lax.rem(seq // 2, 2)
    c = lax.rem(seq, 2)
    other = 1 - c
    z = t * 2 + zl
    low_y = xy < 8

    def at(xy_, z_, c_):
        return (xy_ * 4 + lax.rem(z_, 2) * 2 + c_, z_ // 2)

    sibling = at(xy, z, other)
    partner = at(xy, lax.rem(z + 2, 4), c)

    def plane_dev(j):
        return at(j, z, c)

    def z_dev(z_):
        return at(xy, z_, c)

    def remote(src, dst, ss, rs, dev):
        return pltpu.make_async_remote_copy(
            src_ref=src, dst_ref=dst, send_sem=ss, recv_sem=rs, device_id=dev, device_id_type=MESH
        )

    def sent(shape_of, sem):
        remote(shape_of, shape_of, sem, sem, sibling).wait_send()

    def landed(shape_of, sem):
        remote(shape_of, shape_of, sem, sem, sibling).wait_recv()

    def head_cols(h):
        return pl.ds(pl.multiple_of(h * DH, DH), DH)

    mine = pl.ds(pl.multiple_of(c * WIDE, WIDE), WIDE)
    theirs = pl.ds(pl.multiple_of(other * WIDE, WIDE), WIDE)
    own_rows = pl.ds(HALF, HALF)
    prev_rows = pl.ds(0, HALF)
    all_rows = pl.ds(0, HALF)

    ins = ((k_in, kc, own_rows), (v_in, vc, own_rows), (q_in, qb, all_rows), (g_in, gb, all_rows))
    local_in = [
        pltpu.make_async_copy(src.at[:, mine], buf.at[c, rows, :], in_l.at[i])
        for i, (src, buf, rows) in enumerate(ins)
    ]
    remote_in = [
        remote(src.at[:, theirs], buf.at[c, rows, :], in_s.at[i], in_r.at[i], sibling)
        for i, (src, buf, rows) in enumerate(ins)
    ]
    for copy in local_in:
        copy.start()

    barrier = pltpu.get_barrier_semaphore()
    pl.semaphore_signal(barrier, inc=1, device_id=sibling, device_id_type=MESH)
    for dz in range(1, 4):
        pl.semaphore_signal(barrier, inc=1, device_id=z_dev(lax.rem(z + dz, 4)), device_id_type=MESH)

    @pl.loop(1, PLANE)
    def _(j):
        pl.semaphore_signal(barrier, inc=1, device_id=plane_dev(lax.rem(xy + j, PLANE)), device_id_type=MESH)

    @pl.when(t == 0)
    def _():
        kc[:, 0:HALF, :] = jnp.zeros((2, HALF, WIDE), jnp.bfloat16)
        vc[:, 0:HALF, :] = jnp.zeros((2, HALF, WIDE), jnp.bfloat16)

    st[...] = jnp.zeros_like(st)
    pl.semaphore_wait(barrier, 4 + PLANE - 1)

    def swap_copy(h, own, k, back, fresh):
        cols = head_cols(h)
        p = c if own else other
        if back:
            src, buf, dst, rows, far_rows = (q_in, g_in)[k], (qb, gb)[k], (q1b, g1b)[k], all_rows, all_rows
        else:
            src, buf, dst, rows, far_rows = (k_in, v_in)[k], (kc, vc)[k], (kc, vc)[k], own_rows, prev_rows
        src = src.at[:, head_cols(c * HEADS + h)] if fresh else buf.at[p, rows, cols]
        return remote(src, dst.at[p, far_rows, cols], sw_s, sw_r.at[h], partner)

    def swap(begin, end, sides=(True, False), fresh=False):
        for back in (False, True):

            @pl.when(t == (1 if back else 0))
            def _():
                @pl.loop(begin, end)
                def _(i):
                    h = lax.rem(xy + i, HEADS)
                    for own in sides:
                        for k in range(2):
                            swap_copy(h, own, k, back, fresh).start()

    for copy in remote_in[:2]:
        copy.start()
    swap(0, EARLY, (True,), True)
    for copy in remote_in[2:]:
        copy.start()

    a = anchor[0]
    a_core = lax.rem(a, 2)
    a_zl = lax.rem(a // 2, 2)
    a_xy = a // 4

    for i in range(2):
        local_in[i].wait()
        remote_in[i].wait_recv()

    for kv, buf in enumerate((kc, vc)):
        for h in range(HEADS):
            cols = slice(h * DH, (h + 1) * DH)
            sel[kv * HEADS + h] = jnp.where(
                a_core == 0, buf[0, HALF:BLOCK, cols], buf[1, HALF:BLOCK, cols]
            )

    def s1_copy(j):
        return remote(sel.at[j], cand.at[lax.rem(xy, 8)], s1_s, s1_r, plane_dev(j))

    @pl.when(low_y)
    def _():
        @pl.loop(1, PLANE)
        def _(i):
            s1_copy(lax.rem(xy + i, PLANE)).start()

        cand[lax.rem(xy, 8)] = sel[xy]

    for i in range(2, 4):
        local_in[i].wait()
        remote_in[i].wait_recv()
    swap(0, EARLY, (False,))

    @pl.when(low_y)
    def _():
        landed(cand.at[pl.ds(0, 7)], s1_r)

    @pl.when(jnp.logical_not(low_y))
    def _():
        landed(cand, s1_r)

    zb[z] = cand[a_xy]

    def s2_copy(dz):
        return remote(zb.at[z], zb.at[z], s2_s, s2_r, z_dev(lax.rem(z + dz, 4)))

    for dz in range(1, 4):
        s2_copy(dz).start()
    landed(zb.at[pl.ds(0, 3)], s2_r)
    kva[xy, 0:HALF, :] = zb[a_zl]
    kva[xy, HALF:BLOCK, :] = zb[2 + a_zl]

    x, y = lax.rem(xy, 4), xy // 4

    def along(slot, k, on_x, step):
        dev = y * 4 + lax.rem(x + step, 4) if on_x else lax.rem(y + step, 4) * 4 + x
        part = kva.at[slot, pl.ds(k * HALF, HALF), :]
        return remote(part, part, s3_s, s3_r.at[slot, k], plane_dev(dev))

    def arrived(slot, k):
        landed(kva.at[slot, pl.ds(k * HALF, HALF), :], s3_r.at[slot, k])

    for second_leg in (False, True):
        for step in (1, 3, 2):
            for k in range(2):
                along(xy, k, (k == 0) != second_leg, step).start()

    swap(EARLY, AHEAD)

    for n in (1, 3, 2):
        for k in range(2):
            slot = y * 4 + lax.rem(x + n, 4) if k == 0 else lax.rem(y + n, 4) * 4 + x
            arrived(slot, k)
            for step in (1, 3, 2):
                along(slot, k, k == 1, step).start()

    block0 = seq - c
    row = lax.broadcasted_iota(jnp.int32, (HALF, BLOCK), 0)
    col = lax.broadcasted_iota(jnp.int32, (HALF, BLOCK), 1)
    own_ok = jnp.where(col < HALF, jnp.where(t == 1, 1, 0), jnp.where(row >= col - HALF, 1, 0)) > 0
    own_bias = jnp.where(own_ok, 0.0, LOW)
    own_bias = jnp.concatenate([own_bias, own_bias], 0)
    far_bias = jnp.concatenate(
        [
            jnp.where(col < jnp.where(block0 + p > a, offsets[block0 + p], 0), 0.0, LOW)
            for p in range(2)
        ],
        0,
    )

    def r1_copy(j):
        return remote(fk.at[j], rin.at[xy], r1_s, r1_r, plane_dev(j))

    def st_copy(b):
        return remote(st.at[b], sr.at[b], st_s.at[b], st_r.at[b], partner)

    lane = lax.broadcasted_iota(jnp.int32, (BLOCK, DH), 1)

    @pl.loop(0, HEADS)
    def _(i):
        h = lax.rem(xy + i, HEADS)
        cols = head_cols(h)

        @pl.when(i < HEADS - AHEAD)
        def _():
            swap(i + AHEAD, i + AHEAD + 1)

        for kv in range(2):
            slot = kv * HEADS + h

            @pl.when(slot != xy)
            def _():
                @pl.when(slot // 4 != y)
                def _():
                    arrived(slot, 0)

                @pl.when(lax.rem(slot, 4) != x)
                def _():
                    arrived(slot, 1)

        @pl.when(t == 1)
        def _():
            landed(cand.at[pl.ds(0, 4)], sw_r.at[h])

        q = [qb[p, :, cols] for p in range(2)]
        g = [gb[p, :, cols] for p in range(2)]
        keys = [kc[p, :, cols] for p in range(2)]
        values = [vc[p, :, cols] for p in range(2)]
        q2 = jnp.concatenate(q, 0)
        g2 = jnp.concatenate(g, 0)
        ka = kva[h]
        va = kva[HEADS + h]
        s_far = dot_t(q2, ka) * SCALE + far_bias
        s_own = jnp.concatenate([dot_t(q[p], keys[p]) for p in range(2)], 0) * SCALE + own_bias
        top = jnp.max(jnp.maximum(s_own, s_far), 1, keepdims=True)
        e_own = jnp.exp(s_own - top)
        e_far = jnp.exp(s_far - top)
        total = jnp.sum(e_own + e_far, 1, keepdims=True)
        inv = 1.0 / total
        w_own = e_own.astype(jnp.bfloat16)
        w_far = e_far.astype(jnp.bfloat16)
        w_half = [w_own[p * HALF : (p + 1) * HALF] for p in range(2)]
        mixed = dot(w_far, va) + jnp.concatenate([dot(w_half[p], values[p]) for p in range(2)], 0)
        mixed = mixed * inv
        scaled_g = (g2.astype(jnp.float32) * inv).astype(jnp.bfloat16)
        att = mixed.astype(jnp.bfloat16)
        delta = jnp.sum(g2.astype(jnp.float32) * att.astype(jnp.float32), 1, keepdims=True)
        d_far = (e_far * ((dot_t(g2, va) - delta) * inv)).astype(jnp.bfloat16)
        dp_own = jnp.concatenate([dot_t(g[p], values[p]) for p in range(2)], 0)
        d_own = (e_own * ((dp_own - delta) * inv)).astype(jnp.bfloat16)
        d_half = [d_own[p * HALF : (p + 1) * HALF] for p in range(2)]
        fk[h] = (t_dot(d_far, q2) * SCALE).astype(jnp.bfloat16)
        fk[HEADS + h] = t_dot(w_far, scaled_g).astype(jnp.bfloat16)
        for kv in range(2):
            j = kv * HEADS + h

            @pl.when(j != xy)
            def _():
                r1_copy(j).start()

        batch = i // 4
        place = lax.rem(i, 4) * 4
        stats = st[batch]
        for k, value in enumerate((top, inv, delta)):
            stats = jnp.where(lane == place + k, value, stats)
        st[batch] = stats

        @pl.when(jnp.logical_and(t == 1, lax.rem(i, 4) == 3))
        def _():
            st_copy(batch).start()

        for p in range(2):
            okf[p, :, cols] = t_dot(d_half[p][:, HALF:], q[p]) * SCALE
            ovf[p, :, cols] = t_dot(w_half[p][:, HALF:], scaled_g[p * HALF : (p + 1) * HALF])

        grad_q = dot(d_far, ka) + jnp.concatenate([dot(d_half[p], keys[p]) for p in range(2)], 0)
        grad_q = (grad_q * SCALE).astype(jnp.bfloat16)
        for p in range(2):
            att_b[p, :, cols] = att[p * HALF : (p + 1) * HALF]
            gq_b[p, :, cols] = grad_q[p * HALF : (p + 1) * HALF]

    outs = ((att_b, att_out), (gq_b, gq_out), (gk_b, gk_out), (gv_b, gv_out))
    local_out = [
        pltpu.make_async_copy(buf.at[c], dst.at[:, mine], out_l.at[i]) for i, (buf, dst) in enumerate(outs)
    ]
    remote_out = [
        remote(buf.at[other], dst.at[:, mine], out_s.at[i], out_r.at[i], sibling)
        for i, (buf, dst) in enumerate(outs)
    ]
    for i in range(2):
        remote_out[i].start()
        local_out[i].start()

    def cross(begin, end):
        @pl.when(t == 0)
        def _():
            for b in range(begin // 4, (end + 3) // 4):
                if begin <= 4 * b:
                    st_copy(b).wait_recv()

            @pl.loop(begin, end)
            def _(i):
                h = lax.rem(xy + i, HEADS)
                cols = head_cols(h)
                landed(cand.at[pl.ds(0, 4)], sw_r.at[h])
                stats = sr[i // 4]
                place = lax.rem(i, 4) * 4
                top, inv, delta = [
                    jnp.sum(jnp.where(lane == place + k, stats, 0.0), 1, keepdims=True) for k in range(3)
                ]
                q = [q1b[p, :, cols] for p in range(2)]
                g = [g1b[p, :, cols] for p in range(2)]
                s = jnp.concatenate([dot_t(q[p], kc[p, HALF:BLOCK, cols]) for p in range(2)], 0) * SCALE
                dp = jnp.concatenate([dot_t(g[p], vc[p, HALF:BLOCK, cols]) for p in range(2)], 0)
                prob = jnp.exp(s - top) * inv
                w = prob.astype(jnp.bfloat16)
                d = (prob * (dp - delta)).astype(jnp.bfloat16)
                for p in range(2):
                    rows = slice(p * HALF, (p + 1) * HALF)
                    okf[p, :, cols] += t_dot(d[rows], q[p]) * SCALE
                    ovf[p, :, cols] += t_dot(w[rows], g[p])

    for copy in remote_in:
        copy.wait_send()

    @pl.when(low_y)
    def _():
        sent(sel.at[pl.ds(0, PLANE - 1)], s1_s)

    sent(zb.at[pl.ds(0, 3)], s2_s)
    sent(kva.at[pl.ds(0, PLANE - 1)], s3_s)
    sent(kc, sw_s)

    cross(0, 4)

    landed(rin.at[pl.ds(0, PLANE - 1)], r1_r)
    rin[xy] = fk[xy]
    acc = rin[0].astype(jnp.float32)
    for slot in range(1, PLANE):
        acc = acc + rin[slot].astype(jnp.float32)
    zs[0] = acc[:HALF].astype(jnp.bfloat16)
    zs[1] = acc[HALF:].astype(jnp.bfloat16)

    def r2_copy(dz):
        z_ = lax.rem(z + dz, 4)
        return remote(zs.at[z_ // 2], zr.at[z], r2_s, r2_r, z_dev(z_))

    for dz in range(1, 4):
        r2_copy(dz).start()
    zr[z] = zs[t]
    sent(fk.at[pl.ds(0, PLANE - 1)], r1_s)
    landed(zr.at[pl.ds(0, 3)], r2_r)
    total = zr[0].astype(jnp.float32)
    for slot in range(1, 4):
        total = total + zr[slot].astype(jnp.float32)
    an[...] = total.astype(jnp.bfloat16)

    def r3_copy(j):
        return remote(an, ank.at[xy], r3_s, r3_r, plane_dev(j))

    @pl.loop(0, 8)
    def _(i):
        j = lax.rem(xy + i, 8)

        @pl.when(j != xy)
        def _():
            r3_copy(j).start()

    cross(4, HEADS)
    sent(zr.at[pl.ds(0, 3)], r2_s)

    @pl.when(t == 1)
    def _():
        for b in range(2):
            st_copy(b).wait_send()

    @pl.when(low_y)
    def _():
        ank[xy] = an[...]
        landed(ank.at[pl.ds(0, PLANE - 1)], r3_r)

    for p in (other, c):
        for kv, (grads, out) in enumerate(((okf, gk_b), (ovf, gv_b))):
            owner = block0 + p == a

            @pl.when(low_y)
            def _():
                for h in range(HEADS):
                    cols = slice(h * DH, (h + 1) * DH)
                    far = jnp.where(owner, ank[kv * HEADS + h].astype(jnp.float32), 0.0)
                    out[p, :, cols] = (grads[p, :, cols] + far).astype(jnp.bfloat16)

            @pl.when(jnp.logical_not(low_y))
            def _():
                out[p] = grads[p].astype(jnp.bfloat16)

            if p is other:
                remote_out[2 + kv].start()
            else:
                local_out[2 + kv].start()

    @pl.when(low_y)
    def _():
        sent(ank.at[pl.ds(0, 7)], r3_s)

    @pl.when(jnp.logical_not(low_y))
    def _():
        sent(ank.at[pl.ds(0, 8)], r3_s)

    for copy in local_out:
        copy.wait()
    for copy in remote_out:
        copy.wait()


def write_out(*refs):
    sems, sems2, hold = refs[8:]
    first = [pltpu.make_async_copy(refs[i], hold.at[i], sems.at[i]) for i in range(4)]
    second = [pltpu.make_async_copy(hold.at[i], refs[4 + i], sems2.at[i]) for i in range(4)]
    for copy in first:
        copy.start()
    for i in range(4):
        first[i].wait()
        second[i].start()
    for copy in second:
        copy.wait()


def on_device(queries, key_rows, value_rows, grad_out, anchor, offsets):
    bf16, f32 = jnp.bfloat16, jnp.float32
    any_spec = pl.BlockSpec(memory_space=pl.ANY)
    smem_spec = pl.BlockSpec(memory_space=pltpu.SMEM)
    dma = pltpu.SemaphoreType.DMA
    half = (HALF, DH)
    whole = (BLOCK, DH)
    scratch = [
        pltpu.VMEM((2, HALF, WIDE), bf16),
        pltpu.VMEM((2, HALF, WIDE), bf16),
        pltpu.VMEM((2, BLOCK, WIDE), bf16),
        pltpu.VMEM((2, BLOCK, WIDE), bf16),
        pltpu.VMEM((PLANE, *half), bf16),
        pltpu.VMEM((8, *half), bf16),
        pltpu.VMEM((4, *half), bf16),
        pltpu.VMEM((PLANE, *whole), bf16),
        pltpu.VMEM((PLANE, *whole), bf16),
        pltpu.VMEM((PLANE, *whole), bf16),
        pltpu.VMEM((2, *half), bf16),
        pltpu.VMEM((4, *half), bf16),
        pltpu.VMEM(half, bf16),
        pltpu.VMEM((PLANE, *half), bf16),
        pltpu.VMEM((2, HALF, WIDE), f32),
        pltpu.VMEM((2, HALF, WIDE), f32),
        pltpu.VMEM((2, HALF, WIDE), bf16),
        pltpu.VMEM((2, HALF, WIDE), bf16),
        pltpu.VMEM((2, BLOCK, DH), f32),
        pltpu.VMEM((2, BLOCK, DH), f32),
        pltpu.VMEM((2, HALF, WIDE), bf16),
        pltpu.VMEM((2, HALF, WIDE), bf16),
        pltpu.VMEM((2, HALF, WIDE), bf16),
        pltpu.VMEM((2, HALF, WIDE), bf16),
        dma((4,)), dma((4,)), dma((4,)),
        dma, dma((HEADS,)),
        dma, dma,
        dma, dma,
        dma, dma((PLANE, 2)),
        dma, dma,
        dma, dma,
        dma, dma,
        dma((2,)), dma((2,)),
        dma((4,)), dma((4,)), dma((4,)),
    ]
    results = pl.pallas_call(
        kernel,
        out_shape=[jax.ShapeDtypeStruct(queries.shape, bf16)] * 4,
        in_specs=[smem_spec, smem_spec] + [pl.BlockSpec(memory_space=pltpu.HBM)] * 4,
        out_specs=[any_spec] * 4,
        scratch_shapes=scratch,
        compiler_params=pltpu.CompilerParams(
            collective_id=0, has_side_effects=True, vmem_limit_bytes=60 * 2**20
        ),
        name="anchor_attention",
    )(anchor, offsets, queries, key_rows, value_rows, grad_out)
    return pl.pallas_call(
        write_out,
        out_shape=[jax.ShapeDtypeStruct(queries.shape, bf16)] * 4,
        in_specs=[any_spec] * 4,
        out_specs=[pl.BlockSpec(memory_space=pltpu.HBM)] * 4,
        scratch_shapes=[dma((4,)), dma((4,)), pltpu.VMEM((4, *queries.shape), bf16)],
        name="write_out",
    )(*results)


def solution(mesh):
    tokens = P(("seq", "head"), None)
    return jax.shard_map(
        on_device,
        mesh=mesh,
        in_specs=(tokens, tokens, tokens, tokens, P(), P()),
        out_specs=(tokens, tokens, tokens, tokens),
        check_vma=False,
    )
```

```python
import jax
import jax.numpy as jnp
from jax import lax
from jax.experimental import pallas as pl
from jax.experimental.pallas import tpu as pltpu
from jax.sharding import PartitionSpec as P

DH = 128
BLOCK = 256
HALF = 128
HEADS = 8
WIDE = HEADS * DH
PLANE = 16
SCALE = DH**-0.5
MESH = pl.DeviceIdType.MESH
LOW = -1e30
EARLY = 4
AHEAD = 6


def dot_t(a, b):
    return lax.dot_general(a, b, (((1,), (1,)), ((), ())), preferred_element_type=jnp.float32)


def t_dot(a, b):
    return lax.dot_general(a, b, (((0,), (0,)), ((), ())), preferred_element_type=jnp.float32)


def dot(a, b):
    return jnp.dot(a, b, preferred_element_type=jnp.float32)


def kernel(
    anchor, offsets, q_in, k_in, v_in, g_in,
    att_out, gq_out, gk_out, gv_out,
    qb, gb, kc, vc, sel, cand, zb, kva, fk, rin, zs, zr, an, ank,
    okf, ovf, q1b, g1b, st, sr, att_b, gq_b, gk_b, gv_b,
    in_l, in_s, in_r, sw_s, sw_r, s1_s, s1_r, s2_s, s2_r, s3_s, s3_r,
    r1_s, r1_r, r2_s, r2_r, r3_s, r3_r, st_s, st_r, out_l, out_s, out_r,
):
    seq = lax.axis_index("seq")
    t = lax.axis_index("head")
    xy = seq // 4
    zl = lax.rem(seq // 2, 2)
    c = lax.rem(seq, 2)
    other = 1 - c
    z = t * 2 + zl
    low_y = xy < 8

    def at(xy_, z_, c_):
        return (xy_ * 4 + lax.rem(z_, 2) * 2 + c_, z_ // 2)

    sibling = at(xy, z, other)
    partner = at(xy, lax.rem(z + 2, 4), c)

    def plane_dev(j):
        return at(j, z, c)

    def z_dev(z_):
        return at(xy, z_, c)

    def remote(src, dst, ss, rs, dev):
        return pltpu.make_async_remote_copy(
            src_ref=src, dst_ref=dst, send_sem=ss, recv_sem=rs, device_id=dev, device_id_type=MESH
        )

    def sent(shape_of, sem):
        remote(shape_of, shape_of, sem, sem, sibling).wait_send()

    def landed(shape_of, sem):
        remote(shape_of, shape_of, sem, sem, sibling).wait_recv()

    def head_cols(h):
        return pl.ds(pl.multiple_of(h * DH, DH), DH)

    mine = pl.ds(pl.multiple_of(c * WIDE, WIDE), WIDE)
    theirs = pl.ds(pl.multiple_of(other * WIDE, WIDE), WIDE)
    own_rows = pl.ds(HALF, HALF)
    prev_rows = pl.ds(0, HALF)
    all_rows = pl.ds(0, HALF)

    ins = ((k_in, kc, own_rows), (v_in, vc, own_rows), (q_in, qb, all_rows), (g_in, gb, all_rows))
    local_in = [
        pltpu.make_async_copy(src.at[:, mine], buf.at[c, rows, :], in_l.at[i])
        for i, (src, buf, rows) in enumerate(ins)
    ]
    remote_in = [
        remote(src.at[:, theirs], buf.at[c, rows, :], in_s.at[i], in_r.at[i], sibling)
        for i, (src, buf, rows) in enumerate(ins)
    ]
    for copy in local_in:
        copy.start()

    barrier = pltpu.get_barrier_semaphore()
    pl.semaphore_signal(barrier, inc=1, device_id=sibling, device_id_type=MESH)
    for dz in range(1, 4):
        pl.semaphore_signal(barrier, inc=1, device_id=z_dev(lax.rem(z + dz, 4)), device_id_type=MESH)

    @pl.loop(1, PLANE)
    def _(j):
        pl.semaphore_signal(barrier, inc=1, device_id=plane_dev(lax.rem(xy + j, PLANE)), device_id_type=MESH)

    @pl.when(t == 0)
    def _():
        kc[:, 0:HALF, :] = jnp.zeros((2, HALF, WIDE), jnp.bfloat16)
        vc[:, 0:HALF, :] = jnp.zeros((2, HALF, WIDE), jnp.bfloat16)

    st[...] = jnp.zeros_like(st)
    pl.semaphore_wait(barrier, 4 + PLANE - 1)

    def swap_copy(h, own, k, back, fresh):
        cols = head_cols(h)
        p = c if own else other
        if back:
            src, buf, dst, rows, far_rows = (q_in, g_in)[k], (qb, gb)[k], (q1b, g1b)[k], all_rows, all_rows
        else:
            src, buf, dst, rows, far_rows = (k_in, v_in)[k], (kc, vc)[k], (kc, vc)[k], own_rows, prev_rows
        src = src.at[:, head_cols(c * HEADS + h)] if fresh else buf.at[p, rows, cols]
        return remote(src, dst.at[p, far_rows, cols], sw_s, sw_r.at[h], partner)

    def swap(begin, end, sides=(True, False), fresh=False):
        for back in (False, True):

            @pl.when(t == (1 if back else 0))
            def _():
                @pl.loop(begin, end)
                def _(i):
                    h = lax.rem(xy + i, HEADS)
                    for own in sides:
                        for k in range(2):
                            swap_copy(h, own, k, back, fresh).start()

    for copy in remote_in[:2]:
        copy.start()
    swap(0, EARLY, (True,), True)
    for copy in remote_in[2:]:
        copy.start()

    a = anchor[0]
    a_core = lax.rem(a, 2)
    a_zl = lax.rem(a // 2, 2)
    a_xy = a // 4

    for i in range(2):
        local_in[i].wait()
        remote_in[i].wait_recv()

    for kv, buf in enumerate((kc, vc)):
        for h in range(HEADS):
            cols = slice(h * DH, (h + 1) * DH)
            sel[kv * HEADS + h] = jnp.where(
                a_core == 0, buf[0, HALF:BLOCK, cols], buf[1, HALF:BLOCK, cols]
            )

    def s1_copy(j):
        return remote(sel.at[j], cand.at[lax.rem(xy, 8)], s1_s, s1_r, plane_dev(j))

    @pl.when(low_y)
    def _():
        @pl.loop(1, PLANE)
        def _(i):
            s1_copy(lax.rem(xy + i, PLANE)).start()

        cand[lax.rem(xy, 8)] = sel[xy]

    for i in range(2, 4):
        local_in[i].wait()
        remote_in[i].wait_recv()
    swap(0, EARLY, (False,))

    @pl.when(low_y)
    def _():
        landed(cand.at[pl.ds(0, 7)], s1_r)

    @pl.when(jnp.logical_not(low_y))
    def _():
        landed(cand, s1_r)

    zb[z] = cand[a_xy]

    def s2_copy(dz):
        return remote(zb.at[z], zb.at[z], s2_s, s2_r, z_dev(lax.rem(z + dz, 4)))

    for dz in range(1, 4):
        s2_copy(dz).start()
    landed(zb.at[pl.ds(0, 3)], s2_r)
    kva[xy, 0:HALF, :] = zb[a_zl]
    kva[xy, HALF:BLOCK, :] = zb[2 + a_zl]

    x, y = lax.rem(xy, 4), xy // 4

    def along(slot, k, on_x, step):
        dev = y * 4 + lax.rem(x + step, 4) if on_x else lax.rem(y + step, 4) * 4 + x
        part = kva.at[slot, pl.ds(k * HALF, HALF), :]
        return remote(part, part, s3_s, s3_r.at[slot, k], plane_dev(dev))

    def arrived(slot, k):
        landed(kva.at[slot, pl.ds(k * HALF, HALF), :], s3_r.at[slot, k])

    for second_leg in (False, True):
        for step in (1, 3, 2):
            for k in range(2):
                along(xy, k, (k == 0) != second_leg, step).start()

    swap(EARLY, AHEAD)

    for n in (1, 3, 2):
        for k in range(2):
            slot = y * 4 + lax.rem(x + n, 4) if k == 0 else lax.rem(y + n, 4) * 4 + x
            arrived(slot, k)
            for step in (1, 3, 2):
                along(slot, k, k == 1, step).start()

    block0 = seq - c
    row = lax.broadcasted_iota(jnp.int32, (HALF, BLOCK), 0)
    col = lax.broadcasted_iota(jnp.int32, (HALF, BLOCK), 1)
    own_ok = jnp.where(col < HALF, jnp.where(t == 1, 1, 0), jnp.where(row >= col - HALF, 1, 0)) > 0
    own_bias = jnp.where(own_ok, 0.0, LOW)
    own_bias = jnp.concatenate([own_bias, own_bias], 0)
    far_bias = jnp.concatenate(
        [
            jnp.where(col < jnp.where(block0 + p > a, offsets[block0 + p], 0), 0.0, LOW)
            for p in range(2)
        ],
        0,
    )

    def r1_copy(j):
        return remote(fk.at[j], rin.at[xy], r1_s, r1_r, plane_dev(j))

    def st_copy(b):
        return remote(st.at[b], sr.at[b], st_s.at[b], st_r.at[b], partner)

    lane = lax.broadcasted_iota(jnp.int32, (BLOCK, DH), 1)

    @pl.loop(0, HEADS)
    def _(i):
        h = lax.rem(xy + i, HEADS)
        cols = head_cols(h)

        @pl.when(i < HEADS - AHEAD)
        def _():
            swap(i + AHEAD, i + AHEAD + 1)

        for kv in range(2):
            slot = kv * HEADS + h

            @pl.when(slot != xy)
            def _():
                @pl.when(slot // 4 != y)
                def _():
                    arrived(slot, 0)

                @pl.when(lax.rem(slot, 4) != x)
                def _():
                    arrived(slot, 1)

        @pl.when(t == 1)
        def _():
            landed(cand.at[pl.ds(0, 4)], sw_r.at[h])

        q = [qb[p, :, cols] for p in range(2)]
        g = [gb[p, :, cols] for p in range(2)]
        keys = [kc[p, :, cols] for p in range(2)]
        values = [vc[p, :, cols] for p in range(2)]
        q2 = jnp.concatenate(q, 0)
        g2 = jnp.concatenate(g, 0)
        ka = kva[h]
        va = kva[HEADS + h]
        s_far = dot_t(q2, ka) * SCALE + far_bias
        s_own = jnp.concatenate([dot_t(q[p], keys[p]) for p in range(2)], 0) * SCALE + own_bias
        top = jnp.max(jnp.maximum(s_own, s_far), 1, keepdims=True)
        e_own = jnp.exp(s_own - top)
        e_far = jnp.exp(s_far - top)
        total = jnp.sum(e_own + e_far, 1, keepdims=True)
        inv = 1.0 / total
        p_own = e_own * inv
        p_far = e_far * inv
        w_own = p_own.astype(jnp.bfloat16)
        w_far = p_far.astype(jnp.bfloat16)
        w_half = [w_own[p * HALF : (p + 1) * HALF] for p in range(2)]
        mixed = dot(w_far, va) + jnp.concatenate([dot(w_half[p], values[p]) for p in range(2)], 0)
        att = mixed.astype(jnp.bfloat16)
        delta = jnp.sum(g2.astype(jnp.float32) * att.astype(jnp.float32), 1, keepdims=True)
        d_far = (p_far * (dot_t(g2, va) - delta)).astype(jnp.bfloat16)
        dp_own = jnp.concatenate([dot_t(g[p], values[p]) for p in range(2)], 0)
        d_own = (p_own * (dp_own - delta)).astype(jnp.bfloat16)
        d_half = [d_own[p * HALF : (p + 1) * HALF] for p in range(2)]
        fk[h] = (t_dot(d_far, q2) * SCALE).astype(jnp.bfloat16)
        fk[HEADS + h] = t_dot(w_far, g2).astype(jnp.bfloat16)
        for kv in range(2):
            j = kv * HEADS + h

            @pl.when(j != xy)
            def _():
                r1_copy(j).start()

        batch = i // 4
        place = lax.rem(i, 4) * 4
        stats = st[batch]
        for k, value in enumerate((top, inv, delta)):
            stats = jnp.where(lane == place + k, value, stats)
        st[batch] = stats

        @pl.when(jnp.logical_and(t == 1, lax.rem(i, 4) == 3))
        def _():
            st_copy(batch).start()

        for p in range(2):
            okf[p, :, cols] = t_dot(d_half[p][:, HALF:], q[p]) * SCALE
            ovf[p, :, cols] = t_dot(w_half[p][:, HALF:], g[p])

        grad_q = dot(d_far, ka) + jnp.concatenate([dot(d_half[p], keys[p]) for p in range(2)], 0)
        grad_q = (grad_q * SCALE).astype(jnp.bfloat16)
        for p in range(2):
            att_b[p, :, cols] = att[p * HALF : (p + 1) * HALF]
            gq_b[p, :, cols] = grad_q[p * HALF : (p + 1) * HALF]

    outs = ((att_b, att_out), (gq_b, gq_out), (gk_b, gk_out), (gv_b, gv_out))
    local_out = [
        pltpu.make_async_copy(buf.at[c], dst.at[:, mine], out_l.at[i]) for i, (buf, dst) in enumerate(outs)
    ]
    remote_out = [
        remote(buf.at[other], dst.at[:, mine], out_s.at[i], out_r.at[i], sibling)
        for i, (buf, dst) in enumerate(outs)
    ]
    for i in range(2):
        remote_out[i].start()
        local_out[i].start()

    def cross(begin, end):
        @pl.when(t == 0)
        def _():
            for b in range(begin // 4, (end + 3) // 4):
                if begin <= 4 * b:
                    st_copy(b).wait_recv()

            @pl.loop(begin, end)
            def _(i):
                h = lax.rem(xy + i, HEADS)
                cols = head_cols(h)
                landed(cand.at[pl.ds(0, 4)], sw_r.at[h])
                stats = sr[i // 4]
                place = lax.rem(i, 4) * 4
                top, inv, delta = [
                    jnp.sum(jnp.where(lane == place + k, stats, 0.0), 1, keepdims=True) for k in range(3)
                ]
                q = [q1b[p, :, cols] for p in range(2)]
                g = [g1b[p, :, cols] for p in range(2)]
                s = jnp.concatenate([dot_t(q[p], kc[p, HALF:BLOCK, cols]) for p in range(2)], 0) * SCALE
                dp = jnp.concatenate([dot_t(g[p], vc[p, HALF:BLOCK, cols]) for p in range(2)], 0)
                prob = jnp.exp(s - top) * inv
                w = prob.astype(jnp.bfloat16)
                d = (prob * (dp - delta)).astype(jnp.bfloat16)
                for p in range(2):
                    rows = slice(p * HALF, (p + 1) * HALF)
                    okf[p, :, cols] += t_dot(d[rows], q[p]) * SCALE
                    ovf[p, :, cols] += t_dot(w[rows], g[p])

    for copy in remote_in:
        copy.wait_send()

    @pl.when(low_y)
    def _():
        sent(sel.at[pl.ds(0, PLANE - 1)], s1_s)

    sent(zb.at[pl.ds(0, 3)], s2_s)
    sent(kva.at[pl.ds(0, PLANE - 1)], s3_s)
    sent(kc, sw_s)

    landed(rin.at[pl.ds(0, PLANE - 1)], r1_r)
    rin[xy] = fk[xy]
    acc = rin[0].astype(jnp.float32)
    for slot in range(1, PLANE):
        acc = acc + rin[slot].astype(jnp.float32)
    zs[0] = acc[:HALF].astype(jnp.bfloat16)
    zs[1] = acc[HALF:].astype(jnp.bfloat16)

    def r2_copy(dz):
        z_ = lax.rem(z + dz, 4)
        return remote(zs.at[z_ // 2], zr.at[z], r2_s, r2_r, z_dev(z_))

    for dz in range(1, 4):
        r2_copy(dz).start()
    zr[z] = zs[t]
    cross(0, 4)
    sent(fk.at[pl.ds(0, PLANE - 1)], r1_s)
    landed(zr.at[pl.ds(0, 3)], r2_r)
    total = zr[0].astype(jnp.float32)
    for slot in range(1, 4):
        total = total + zr[slot].astype(jnp.float32)
    an[...] = total.astype(jnp.bfloat16)

    def r3_copy(j):
        return remote(an, ank.at[xy], r3_s, r3_r, plane_dev(j))

    @pl.loop(0, 8)
    def _(i):
        j = lax.rem(xy + i, 8)

        @pl.when(j != xy)
        def _():
            r3_copy(j).start()

    cross(4, HEADS)
    sent(zr.at[pl.ds(0, 3)], r2_s)

    @pl.when(t == 1)
    def _():
        for b in range(2):
            st_copy(b).wait_send()

    @pl.when(low_y)
    def _():
        ank[xy] = an[...]
        landed(ank.at[pl.ds(0, PLANE - 1)], r3_r)

    for p in (other, c):
        for kv, (grads, out) in enumerate(((okf, gk_b), (ovf, gv_b))):
            owner = block0 + p == a

            @pl.when(low_y)
            def _():
                for h in range(HEADS):
                    cols = slice(h * DH, (h + 1) * DH)
                    far = jnp.where(owner, ank[kv * HEADS + h].astype(jnp.float32), 0.0)
                    out[p, :, cols] = (grads[p, :, cols] + far).astype(jnp.bfloat16)

            @pl.when(jnp.logical_not(low_y))
            def _():
                out[p] = grads[p].astype(jnp.bfloat16)

            if p is other:
                remote_out[2 + kv].start()
            else:
                local_out[2 + kv].start()

    @pl.when(low_y)
    def _():
        sent(ank.at[pl.ds(0, 7)], r3_s)

    @pl.when(jnp.logical_not(low_y))
    def _():
        sent(ank.at[pl.ds(0, 8)], r3_s)

    for copy in local_out:
        copy.wait()
    for copy in remote_out:
        copy.wait()


def write_out(*refs):
    sems, sems2, hold = refs[8:]
    first = [pltpu.make_async_copy(refs[i], hold.at[i], sems.at[i]) for i in range(4)]
    second = [pltpu.make_async_copy(hold.at[i], refs[4 + i], sems2.at[i]) for i in range(4)]
    for copy in first:
        copy.start()
    for i in range(4):
        first[i].wait()
        second[i].start()
    for copy in second:
        copy.wait()


def on_device(queries, key_rows, value_rows, grad_out, anchor, offsets):
    bf16, f32 = jnp.bfloat16, jnp.float32
    any_spec = pl.BlockSpec(memory_space=pl.ANY)
    smem_spec = pl.BlockSpec(memory_space=pltpu.SMEM)
    dma = pltpu.SemaphoreType.DMA
    half = (HALF, DH)
    whole = (BLOCK, DH)
    scratch = [
        pltpu.VMEM((2, HALF, WIDE), bf16),
        pltpu.VMEM((2, HALF, WIDE), bf16),
        pltpu.VMEM((2, BLOCK, WIDE), bf16),
        pltpu.VMEM((2, BLOCK, WIDE), bf16),
        pltpu.VMEM((PLANE, *half), bf16),
        pltpu.VMEM((8, *half), bf16),
        pltpu.VMEM((4, *half), bf16),
        pltpu.VMEM((PLANE, *whole), bf16),
        pltpu.VMEM((PLANE, *whole), bf16),
        pltpu.VMEM((PLANE, *whole), bf16),
        pltpu.VMEM((2, *half), bf16),
        pltpu.VMEM((4, *half), bf16),
        pltpu.VMEM(half, bf16),
        pltpu.VMEM((PLANE, *half), bf16),
        pltpu.VMEM((2, HALF, WIDE), f32),
        pltpu.VMEM((2, HALF, WIDE), f32),
        pltpu.VMEM((2, HALF, WIDE), bf16),
        pltpu.VMEM((2, HALF, WIDE), bf16),
        pltpu.VMEM((2, BLOCK, DH), f32),
        pltpu.VMEM((2, BLOCK, DH), f32),
        pltpu.VMEM((2, HALF, WIDE), bf16),
        pltpu.VMEM((2, HALF, WIDE), bf16),
        pltpu.VMEM((2, HALF, WIDE), bf16),
        pltpu.VMEM((2, HALF, WIDE), bf16),
        dma((4,)), dma((4,)), dma((4,)),
        dma, dma((HEADS,)),
        dma, dma,
        dma, dma,
        dma, dma((PLANE, 2)),
        dma, dma,
        dma, dma,
        dma, dma,
        dma((2,)), dma((2,)),
        dma((4,)), dma((4,)), dma((4,)),
    ]
    results = pl.pallas_call(
        kernel,
        out_shape=[jax.ShapeDtypeStruct(queries.shape, bf16)] * 4,
        in_specs=[smem_spec, smem_spec] + [pl.BlockSpec(memory_space=pltpu.HBM)] * 4,
        out_specs=[any_spec] * 4,
        scratch_shapes=scratch,
        compiler_params=pltpu.CompilerParams(
            collective_id=0, has_side_effects=True, vmem_limit_bytes=60 * 2**20
        ),
        name="anchor_attention",
    )(anchor, offsets, queries, key_rows, value_rows, grad_out)
    return pl.pallas_call(
        write_out,
        out_shape=[jax.ShapeDtypeStruct(queries.shape, bf16)] * 4,
        in_specs=[any_spec] * 4,
        out_specs=[pl.BlockSpec(memory_space=pltpu.HBM)] * 4,
        scratch_shapes=[dma((4,)), dma((4,)), pltpu.VMEM((4, *queries.shape), bf16)],
        name="write_out",
    )(*results)


def solution(mesh):
    tokens = P(("seq", "head"), None)
    return jax.shard_map(
        on_device,
        mesh=mesh,
        in_specs=(tokens, tokens, tokens, tokens, P(), P()),
        out_specs=(tokens, tokens, tokens, tokens),
        check_vma=False,
    )
```

```python
import jax
import jax.numpy as jnp
from jax import lax
from jax.experimental import pallas as pl
from jax.experimental.pallas import tpu as pltpu
from jax.sharding import PartitionSpec as P

DH = 128
BLOCK = 256
HALF = 128
HEADS = 8
WIDE = HEADS * DH
PLANE = 16
SCALE = DH**-0.5
MESH = pl.DeviceIdType.MESH
LOW = -1e30
EARLY_OWN = 5
EARLY = 3
AHEAD = 5


def dot_t(a, b):
    return lax.dot_general(a, b, (((1,), (1,)), ((), ())), preferred_element_type=jnp.float32)


def t_dot(a, b):
    return lax.dot_general(a, b, (((0,), (0,)), ((), ())), preferred_element_type=jnp.float32)


def dot(a, b):
    return jnp.dot(a, b, preferred_element_type=jnp.float32)


def kernel(
    anchor, offsets, q_in, k_in, v_in, g_in,
    att_out, gq_out, gk_out, gv_out,
    qb, gb, kc, vc, sel, cand, zb, kva, fk, rin, zs, zr, an, ank,
    okf, ovf, q1b, g1b, st, sr, att_b, gq_b, gk_b, gv_b,
    in_l, in_s, in_r, sw_s, sw_r, s1_s, s1_r, s2_s, s2_r, s3_s, s3_r,
    r1_s, r1_r, r2_s, r2_r, r3_s, r3_r, st_s, st_r, out_l, out_s, out_r,
):
    seq = lax.axis_index("seq")
    t = lax.axis_index("head")
    xy = seq // 4
    zl = lax.rem(seq // 2, 2)
    c = lax.rem(seq, 2)
    other = 1 - c
    z = t * 2 + zl
    low_y = xy < 8

    def at(xy_, z_, c_):
        return (xy_ * 4 + lax.rem(z_, 2) * 2 + c_, z_ // 2)

    sibling = at(xy, z, other)
    partner = at(xy, lax.rem(z + 2, 4), c)

    def plane_dev(j):
        return at(j, z, c)

    def z_dev(z_):
        return at(xy, z_, c)

    def remote(src, dst, ss, rs, dev):
        return pltpu.make_async_remote_copy(
            src_ref=src, dst_ref=dst, send_sem=ss, recv_sem=rs, device_id=dev, device_id_type=MESH
        )

    def sent(shape_of, sem):
        remote(shape_of, shape_of, sem, sem, sibling).wait_send()

    def landed(shape_of, sem):
        remote(shape_of, shape_of, sem, sem, sibling).wait_recv()

    def head_cols(h):
        return pl.ds(pl.multiple_of(h * DH, DH), DH)

    mine = pl.ds(pl.multiple_of(c * WIDE, WIDE), WIDE)
    theirs = pl.ds(pl.multiple_of(other * WIDE, WIDE), WIDE)
    own_rows = pl.ds(HALF, HALF)
    prev_rows = pl.ds(0, HALF)
    all_rows = pl.ds(0, HALF)

    ins = ((k_in, kc, own_rows), (v_in, vc, own_rows), (q_in, qb, all_rows), (g_in, gb, all_rows))
    local_in = [
        pltpu.make_async_copy(src.at[:, mine], buf.at[c, rows, :], in_l.at[i])
        for i, (src, buf, rows) in enumerate(ins)
    ]
    remote_in = [
        remote(src.at[:, theirs], buf.at[c, rows, :], in_s.at[i], in_r.at[i], sibling)
        for i, (src, buf, rows) in enumerate(ins)
    ]
    for copy in local_in:
        copy.start()

    barrier = pltpu.get_barrier_semaphore()
    pl.semaphore_signal(barrier, inc=1, device_id=sibling, device_id_type=MESH)
    for dz in range(1, 4):
        pl.semaphore_signal(barrier, inc=1, device_id=z_dev(lax.rem(z + dz, 4)), device_id_type=MESH)

    @pl.loop(1, PLANE)
    def _(j):
        pl.semaphore_signal(barrier, inc=1, device_id=plane_dev(lax.rem(xy + j, PLANE)), device_id_type=MESH)

    @pl.when(t == 0)
    def _():
        kc[:, 0:HALF, :] = jnp.zeros((2, HALF, WIDE), jnp.bfloat16)
        vc[:, 0:HALF, :] = jnp.zeros((2, HALF, WIDE), jnp.bfloat16)

    st[...] = jnp.zeros_like(st)
    pl.semaphore_wait(barrier, 4 + PLANE - 1)

    def swap_copy(h, own, k, back, fresh):
        cols = head_cols(h)
        p = c if own else other
        if back:
            src, buf, dst, rows, far_rows = (q_in, g_in)[k], (qb, gb)[k], (q1b, g1b)[k], all_rows, all_rows
        else:
            src, buf, dst, rows, far_rows = (k_in, v_in)[k], (kc, vc)[k], (kc, vc)[k], own_rows, prev_rows
        src = src.at[:, head_cols(c * HEADS + h)] if fresh else buf.at[p, rows, cols]
        return remote(src, dst.at[p, far_rows, cols], sw_s, sw_r.at[h], partner)

    def swap(begin, end, sides=(True, False), fresh=False):
        for back in (False, True):

            @pl.when(t == (1 if back else 0))
            def _():
                @pl.loop(begin, end)
                def _(i):
                    h = lax.rem(xy + i, HEADS)
                    for own in sides:
                        for k in range(2):
                            swap_copy(h, own, k, back, fresh).start()

    for copy in remote_in[:2]:
        copy.start()
    swap(0, EARLY_OWN, (True,), True)
    for copy in remote_in[2:]:
        copy.start()

    a = anchor[0]
    a_core = lax.rem(a, 2)
    a_zl = lax.rem(a // 2, 2)
    a_xy = a // 4

    for i in range(2):
        local_in[i].wait()
        remote_in[i].wait_recv()

    for kv, buf in enumerate((kc, vc)):
        for h in range(HEADS):
            cols = slice(h * DH, (h + 1) * DH)
            sel[kv * HEADS + h] = jnp.where(
                a_core == 0, buf[0, HALF:BLOCK, cols], buf[1, HALF:BLOCK, cols]
            )

    def s1_copy(j):
        return remote(sel.at[j], cand.at[lax.rem(xy, 8)], s1_s, s1_r, plane_dev(j))

    @pl.when(low_y)
    def _():
        @pl.loop(1, PLANE)
        def _(i):
            s1_copy(lax.rem(xy + i, PLANE)).start()

        cand[lax.rem(xy, 8)] = sel[xy]

    for i in range(2, 4):
        local_in[i].wait()
        remote_in[i].wait_recv()
    swap(0, EARLY, (False,))

    @pl.when(low_y)
    def _():
        landed(cand.at[pl.ds(0, 7)], s1_r)

    @pl.when(jnp.logical_not(low_y))
    def _():
        landed(cand, s1_r)

    zb[z] = cand[a_xy]

    def s2_copy(dz):
        return remote(zb.at[z], zb.at[z], s2_s, s2_r, z_dev(lax.rem(z + dz, 4)))

    for dz in range(1, 4):
        s2_copy(dz).start()
    landed(zb.at[pl.ds(0, 3)], s2_r)
    kva[xy, 0:HALF, :] = zb[a_zl]
    kva[xy, HALF:BLOCK, :] = zb[2 + a_zl]

    x, y = lax.rem(xy, 4), xy // 4

    def along(slot, k, on_x, step):
        dev = y * 4 + lax.rem(x + step, 4) if on_x else lax.rem(y + step, 4) * 4 + x
        part = kva.at[slot, pl.ds(k * HALF, HALF), :]
        return remote(part, part, s3_s, s3_r.at[slot, k], plane_dev(dev))

    def arrived(slot, k):
        landed(kva.at[slot, pl.ds(k * HALF, HALF), :], s3_r.at[slot, k])

    for second_leg in (False, True):
        for step in (1, 3, 2):
            for k in range(2):
                along(xy, k, (k == 0) != second_leg, step).start()

    swap(EARLY, AHEAD, (False,))
    swap(EARLY_OWN, AHEAD, (True,))

    for n in (1, 3, 2):
        for k in range(2):
            slot = y * 4 + lax.rem(x + n, 4) if k == 0 else lax.rem(y + n, 4) * 4 + x
            arrived(slot, k)
            for step in (1, 3, 2):
                along(slot, k, k == 1, step).start()

    block0 = seq - c
    row = lax.broadcasted_iota(jnp.int32, (HALF, BLOCK), 0)
    col = lax.broadcasted_iota(jnp.int32, (HALF, BLOCK), 1)
    own_ok = jnp.where(col < HALF, jnp.where(t == 1, 1, 0), jnp.where(row >= col - HALF, 1, 0)) > 0
    own_bias = jnp.where(own_ok, 0.0, LOW)
    own_bias = jnp.concatenate([own_bias, own_bias], 0)
    far_bias = jnp.concatenate(
        [
            jnp.where(col < jnp.where(block0 + p > a, offsets[block0 + p], 0), 0.0, LOW)
            for p in range(2)
        ],
        0,
    )

    def r1_copy(j):
        return remote(fk.at[j], rin.at[xy], r1_s, r1_r, plane_dev(j))

    def st_copy(b):
        return remote(st.at[b], sr.at[b], st_s.at[b], st_r.at[b], partner)

    lane = lax.broadcasted_iota(jnp.int32, (BLOCK, DH), 1)

    @pl.loop(0, HEADS)
    def _(i):
        h = lax.rem(xy + i, HEADS)
        cols = head_cols(h)

        @pl.when(i < HEADS - AHEAD)
        def _():
            swap(i + AHEAD, i + AHEAD + 1)

        for kv in range(2):
            slot = kv * HEADS + h

            @pl.when(slot != xy)
            def _():
                @pl.when(slot // 4 != y)
                def _():
                    arrived(slot, 0)

                @pl.when(lax.rem(slot, 4) != x)
                def _():
                    arrived(slot, 1)

        @pl.when(t == 1)
        def _():
            landed(cand.at[pl.ds(0, 4)], sw_r.at[h])

        q = [qb[p, :, cols] for p in range(2)]
        g = [gb[p, :, cols] for p in range(2)]
        keys = [kc[p, :, cols] for p in range(2)]
        values = [vc[p, :, cols] for p in range(2)]
        q2 = jnp.concatenate(q, 0)
        g2 = jnp.concatenate(g, 0)
        ka = kva[h]
        va = kva[HEADS + h]
        s_far = dot_t(q2, ka) * SCALE + far_bias
        s_own = jnp.concatenate([dot_t(q[p], keys[p]) for p in range(2)], 0) * SCALE + own_bias
        top = jnp.max(jnp.maximum(s_own, s_far), 1, keepdims=True)
        e_own = jnp.exp(s_own - top)
        e_far = jnp.exp(s_far - top)
        total = jnp.sum(e_own + e_far, 1, keepdims=True)
        inv = 1.0 / total
        w_own = e_own.astype(jnp.bfloat16)
        w_far = e_far.astype(jnp.bfloat16)
        w_half = [w_own[p * HALF : (p + 1) * HALF] for p in range(2)]
        mixed = dot(w_far, va) + jnp.concatenate([dot(w_half[p], values[p]) for p in range(2)], 0)
        mixed = mixed * inv
        scaled_g = (g2.astype(jnp.float32) * inv).astype(jnp.bfloat16)
        att = mixed.astype(jnp.bfloat16)
        delta = jnp.sum(g2.astype(jnp.float32) * att.astype(jnp.float32), 1, keepdims=True)
        d_far = (e_far * ((dot_t(g2, va) - delta) * inv)).astype(jnp.bfloat16)
        dp_own = jnp.concatenate([dot_t(g[p], values[p]) for p in range(2)], 0)
        d_own = (e_own * ((dp_own - delta) * inv)).astype(jnp.bfloat16)
        d_half = [d_own[p * HALF : (p + 1) * HALF] for p in range(2)]
        fk[h] = (t_dot(d_far, q2) * SCALE).astype(jnp.bfloat16)
        fk[HEADS + h] = t_dot(w_far, scaled_g).astype(jnp.bfloat16)
        for kv in range(2):
            j = kv * HEADS + h

            @pl.when(j != xy)
            def _():
                r1_copy(j).start()

        batch = i // 4
        place = lax.rem(i, 4) * 4
        stats = st[batch]
        for k, value in enumerate((top, inv, delta)):
            stats = jnp.where(lane == place + k, value, stats)
        st[batch] = stats

        @pl.when(jnp.logical_and(t == 1, lax.rem(i, 4) == 3))
        def _():
            st_copy(batch).start()

        for p in range(2):
            okf[p, :, cols] = t_dot(d_half[p][:, HALF:], q[p]) * SCALE
            ovf[p, :, cols] = t_dot(w_half[p][:, HALF:], scaled_g[p * HALF : (p + 1) * HALF])

        grad_q = dot(d_far, ka) + jnp.concatenate([dot(d_half[p], keys[p]) for p in range(2)], 0)
        grad_q = (grad_q * SCALE).astype(jnp.bfloat16)
        for p in range(2):
            att_b[p, :, cols] = att[p * HALF : (p + 1) * HALF]
            gq_b[p, :, cols] = grad_q[p * HALF : (p + 1) * HALF]

    outs = ((att_b, att_out), (gq_b, gq_out), (gk_b, gk_out), (gv_b, gv_out))
    local_out = [
        pltpu.make_async_copy(buf.at[c], dst.at[:, mine], out_l.at[i]) for i, (buf, dst) in enumerate(outs)
    ]
    remote_out = [
        remote(buf.at[other], dst.at[:, mine], out_s.at[i], out_r.at[i], sibling)
        for i, (buf, dst) in enumerate(outs)
    ]
    for i in range(2):
        remote_out[i].start()
        local_out[i].start()

    def cross(begin, end):
        @pl.when(t == 0)
        def _():
            for b in range(begin // 4, (end + 3) // 4):
                if begin <= 4 * b:
                    st_copy(b).wait_recv()

            @pl.loop(begin, end)
            def _(i):
                h = lax.rem(xy + i, HEADS)
                cols = head_cols(h)
                landed(cand.at[pl.ds(0, 4)], sw_r.at[h])
                stats = sr[i // 4]
                place = lax.rem(i, 4) * 4
                top, inv, delta = [
                    jnp.sum(jnp.where(lane == place + k, stats, 0.0), 1, keepdims=True) for k in range(3)
                ]
                q = [q1b[p, :, cols] for p in range(2)]
                g = [g1b[p, :, cols] for p in range(2)]
                s = jnp.concatenate([dot_t(q[p], kc[p, HALF:BLOCK, cols]) for p in range(2)], 0) * SCALE
                dp = jnp.concatenate([dot_t(g[p], vc[p, HALF:BLOCK, cols]) for p in range(2)], 0)
                prob = jnp.exp(s - top) * inv
                w = prob.astype(jnp.bfloat16)
                d = (prob * (dp - delta)).astype(jnp.bfloat16)
                for p in range(2):
                    rows = slice(p * HALF, (p + 1) * HALF)
                    okf[p, :, cols] += t_dot(d[rows], q[p]) * SCALE
                    ovf[p, :, cols] += t_dot(w[rows], g[p])

    for copy in remote_in:
        copy.wait_send()

    @pl.when(low_y)
    def _():
        sent(sel.at[pl.ds(0, PLANE - 1)], s1_s)

    sent(zb.at[pl.ds(0, 3)], s2_s)
    sent(kva.at[pl.ds(0, PLANE - 1)], s3_s)
    sent(kc, sw_s)

    landed(rin.at[pl.ds(0, PLANE - 1)], r1_r)
    rin[xy] = fk[xy]
    acc = rin[0].astype(jnp.float32)
    for slot in range(1, PLANE):
        acc = acc + rin[slot].astype(jnp.float32)
    zs[0] = acc[:HALF].astype(jnp.bfloat16)
    zs[1] = acc[HALF:].astype(jnp.bfloat16)

    def r2_copy(dz):
        z_ = lax.rem(z + dz, 4)
        return remote(zs.at[z_ // 2], zr.at[z], r2_s, r2_r, z_dev(z_))

    for dz in range(1, 4):
        r2_copy(dz).start()
    zr[z] = zs[t]
    cross(0, 4)
    sent(fk.at[pl.ds(0, PLANE - 1)], r1_s)
    landed(zr.at[pl.ds(0, 3)], r2_r)
    total = zr[0].astype(jnp.float32)
    for slot in range(1, 4):
        total = total + zr[slot].astype(jnp.float32)
    an[...] = total.astype(jnp.bfloat16)

    def r3_copy(j):
        return remote(an, ank.at[xy], r3_s, r3_r, plane_dev(j))

    @pl.loop(0, 8)
    def _(i):
        j = lax.rem(xy + i, 8)

        @pl.when(j != xy)
        def _():
            r3_copy(j).start()

    cross(4, HEADS)
    sent(zr.at[pl.ds(0, 3)], r2_s)

    @pl.when(t == 1)
    def _():
        for b in range(2):
            st_copy(b).wait_send()

    @pl.when(low_y)
    def _():
        ank[xy] = an[...]
        landed(ank.at[pl.ds(0, PLANE - 1)], r3_r)

    for p in (other, c):
        for kv, (grads, out) in enumerate(((okf, gk_b), (ovf, gv_b))):
            owner = block0 + p == a

            @pl.when(low_y)
            def _():
                for h in range(HEADS):
                    cols = slice(h * DH, (h + 1) * DH)
                    far = jnp.where(owner, ank[kv * HEADS + h].astype(jnp.float32), 0.0)
                    out[p, :, cols] = (grads[p, :, cols] + far).astype(jnp.bfloat16)

            @pl.when(jnp.logical_not(low_y))
            def _():
                out[p] = grads[p].astype(jnp.bfloat16)

            if p is other:
                remote_out[2 + kv].start()
            else:
                local_out[2 + kv].start()

    @pl.when(low_y)
    def _():
        sent(ank.at[pl.ds(0, 7)], r3_s)

    @pl.when(jnp.logical_not(low_y))
    def _():
        sent(ank.at[pl.ds(0, 8)], r3_s)

    for copy in local_out:
        copy.wait()
    for copy in remote_out:
        copy.wait()


def write_out(*refs):
    sems, sems2, hold = refs[8:]
    first = [pltpu.make_async_copy(refs[i], hold.at[i], sems.at[i]) for i in range(4)]
    second = [pltpu.make_async_copy(hold.at[i], refs[4 + i], sems2.at[i]) for i in range(4)]
    for copy in first:
        copy.start()
    for i in range(4):
        first[i].wait()
        second[i].start()
    for copy in second:
        copy.wait()


def on_device(queries, key_rows, value_rows, grad_out, anchor, offsets):
    bf16, f32 = jnp.bfloat16, jnp.float32
    any_spec = pl.BlockSpec(memory_space=pl.ANY)
    smem_spec = pl.BlockSpec(memory_space=pltpu.SMEM)
    dma = pltpu.SemaphoreType.DMA
    half = (HALF, DH)
    whole = (BLOCK, DH)
    scratch = [
        pltpu.VMEM((2, HALF, WIDE), bf16),
        pltpu.VMEM((2, HALF, WIDE), bf16),
        pltpu.VMEM((2, BLOCK, WIDE), bf16),
        pltpu.VMEM((2, BLOCK, WIDE), bf16),
        pltpu.VMEM((PLANE, *half), bf16),
        pltpu.VMEM((8, *half), bf16),
        pltpu.VMEM((4, *half), bf16),
        pltpu.VMEM((PLANE, *whole), bf16),
        pltpu.VMEM((PLANE, *whole), bf16),
        pltpu.VMEM((PLANE, *whole), bf16),
        pltpu.VMEM((2, *half), bf16),
        pltpu.VMEM((4, *half), bf16),
        pltpu.VMEM(half, bf16),
        pltpu.VMEM((PLANE, *half), bf16),
        pltpu.VMEM((2, HALF, WIDE), f32),
        pltpu.VMEM((2, HALF, WIDE), f32),
        pltpu.VMEM((2, HALF, WIDE), bf16),
        pltpu.VMEM((2, HALF, WIDE), bf16),
        pltpu.VMEM((2, BLOCK, DH), f32),
        pltpu.VMEM((2, BLOCK, DH), f32),
        pltpu.VMEM((2, HALF, WIDE), bf16),
        pltpu.VMEM((2, HALF, WIDE), bf16),
        pltpu.VMEM((2, HALF, WIDE), bf16),
        pltpu.VMEM((2, HALF, WIDE), bf16),
        dma((4,)), dma((4,)), dma((4,)),
        dma, dma((HEADS,)),
        dma, dma,
        dma, dma,
        dma, dma((PLANE, 2)),
        dma, dma,
        dma, dma,
        dma, dma,
        dma((2,)), dma((2,)),
        dma((4,)), dma((4,)), dma((4,)),
    ]
    results = pl.pallas_call(
        kernel,
        out_shape=[jax.ShapeDtypeStruct(queries.shape, bf16)] * 4,
        in_specs=[smem_spec, smem_spec] + [pl.BlockSpec(memory_space=pltpu.HBM)] * 4,
        out_specs=[any_spec] * 4,
        scratch_shapes=scratch,
        compiler_params=pltpu.CompilerParams(
            collective_id=0, has_side_effects=True, vmem_limit_bytes=60 * 2**20
        ),
        name="anchor_attention",
    )(anchor, offsets, queries, key_rows, value_rows, grad_out)
    return pl.pallas_call(
        write_out,
        out_shape=[jax.ShapeDtypeStruct(queries.shape, bf16)] * 4,
        in_specs=[any_spec] * 4,
        out_specs=[pl.BlockSpec(memory_space=pltpu.HBM)] * 4,
        scratch_shapes=[dma((4,)), dma((4,)), pltpu.VMEM((4, *queries.shape), bf16)],
        name="write_out",
    )(*results)


def solution(mesh):
    tokens = P(("seq", "head"), None)
    return jax.shard_map(
        on_device,
        mesh=mesh,
        in_specs=(tokens, tokens, tokens, tokens, P(), P()),
        out_specs=(tokens, tokens, tokens, tokens),
        check_vma=False,
    )
```

```python
import jax
import jax.numpy as jnp
from jax import lax
from jax.experimental import pallas as pl
from jax.experimental.pallas import tpu as pltpu
from jax.sharding import PartitionSpec as P

DH = 128
BLOCK = 256
HALF = 128
HEADS = 8
WIDE = HEADS * DH
PLANE = 16
SCALE = DH**-0.5
MESH = pl.DeviceIdType.MESH
LOW = -1e30
EARLY_OWN = 5
EARLY = 3
AHEAD = 5


def dot_t(a, b):
    return lax.dot_general(a, b, (((1,), (1,)), ((), ())), preferred_element_type=jnp.float32)


def t_dot(a, b):
    return lax.dot_general(a, b, (((0,), (0,)), ((), ())), preferred_element_type=jnp.float32)


def dot(a, b):
    return jnp.dot(a, b, preferred_element_type=jnp.float32)


def kernel(
    anchor, offsets, q_in, k_in, v_in, g_in,
    att_out, gq_out, gk_out, gv_out,
    qb, gb, kc, vc, sel, cand, zb, kva, fk, rin, zs, zr, an, ank,
    okf, ovf, q1b, g1b, st, sr, att_b, gq_b, gk_b, gv_b,
    in_l, in_s, in_r, sw_s, sw_r, s1_s, s1_r, s2_s, s2_r, s3_s, s3_r,
    r1_s, r1_r, r2_s, r2_r, r3_s, r3_r, st_s, st_r, out_l, out_s, out_r,
):
    seq = lax.axis_index("seq")
    t = lax.axis_index("head")
    xy = seq // 4
    zl = lax.rem(seq // 2, 2)
    c = lax.rem(seq, 2)
    other = 1 - c
    z = t * 2 + zl
    low_y = xy < 8

    def at(xy_, z_, c_):
        return (xy_ * 4 + lax.rem(z_, 2) * 2 + c_, z_ // 2)

    sibling = at(xy, z, other)
    partner = at(xy, lax.rem(z + 2, 4), c)

    def plane_dev(j):
        return at(j, z, c)

    def z_dev(z_):
        return at(xy, z_, c)

    def remote(src, dst, ss, rs, dev):
        return pltpu.make_async_remote_copy(
            src_ref=src, dst_ref=dst, send_sem=ss, recv_sem=rs, device_id=dev, device_id_type=MESH
        )

    def sent(shape_of, sem):
        remote(shape_of, shape_of, sem, sem, sibling).wait_send()

    def landed(shape_of, sem):
        remote(shape_of, shape_of, sem, sem, sibling).wait_recv()

    def head_cols(h):
        return pl.ds(pl.multiple_of(h * DH, DH), DH)

    mine = pl.ds(pl.multiple_of(c * WIDE, WIDE), WIDE)
    theirs = pl.ds(pl.multiple_of(other * WIDE, WIDE), WIDE)
    own_rows = pl.ds(HALF, HALF)
    prev_rows = pl.ds(0, HALF)
    all_rows = pl.ds(0, HALF)

    ins = ((k_in, kc, own_rows), (v_in, vc, own_rows), (q_in, qb, all_rows), (g_in, gb, all_rows))
    local_in = [
        pltpu.make_async_copy(src.at[:, mine], buf.at[c, rows, :], in_l.at[i])
        for i, (src, buf, rows) in enumerate(ins)
    ]
    remote_in = [
        remote(src.at[:, theirs], buf.at[c, rows, :], in_s.at[i], in_r.at[i], sibling)
        for i, (src, buf, rows) in enumerate(ins)
    ]
    for copy in local_in:
        copy.start()

    barrier = pltpu.get_barrier_semaphore()
    pl.semaphore_signal(barrier, inc=1, device_id=sibling, device_id_type=MESH)
    for dz in range(1, 4):
        pl.semaphore_signal(barrier, inc=1, device_id=z_dev(lax.rem(z + dz, 4)), device_id_type=MESH)

    @pl.loop(1, PLANE)
    def _(j):
        pl.semaphore_signal(barrier, inc=1, device_id=plane_dev(lax.rem(xy + j, PLANE)), device_id_type=MESH)

    @pl.when(t == 0)
    def _():
        kc[:, 0:HALF, :] = jnp.zeros((2, HALF, WIDE), jnp.bfloat16)
        vc[:, 0:HALF, :] = jnp.zeros((2, HALF, WIDE), jnp.bfloat16)

    st[...] = jnp.zeros_like(st)
    pl.semaphore_wait(barrier, 4 + PLANE - 1)

    def swap_copy(h, own, k, back, fresh):
        cols = head_cols(h)
        p = c if own else other
        if back:
            src, buf, dst, rows, far_rows = (q_in, g_in)[k], (qb, gb)[k], (q1b, g1b)[k], all_rows, all_rows
        else:
            src, buf, dst, rows, far_rows = (k_in, v_in)[k], (kc, vc)[k], (kc, vc)[k], own_rows, prev_rows
        src = src.at[:, head_cols(c * HEADS + h)] if fresh else buf.at[p, rows, cols]
        return remote(src, dst.at[p, far_rows, cols], sw_s, sw_r.at[h], partner)

    def swap(begin, end, sides=(True, False), fresh=False):
        for back in (False, True):

            @pl.when(t == (1 if back else 0))
            def _():
                @pl.loop(begin, end)
                def _(i):
                    h = lax.rem(xy + i, HEADS)
                    for own in sides:
                        for k in range(2):
                            swap_copy(h, own, k, back, fresh).start()

    for copy in remote_in[:2]:
        copy.start()
    swap(0, EARLY_OWN, (True,), True)
    for copy in remote_in[2:]:
        copy.start()

    a = anchor[0]
    a_core = lax.rem(a, 2)
    a_zl = lax.rem(a // 2, 2)
    a_xy = a // 4

    for i in range(2):
        local_in[i].wait()
        remote_in[i].wait_recv()

    for kv, buf in enumerate((kc, vc)):
        for h in range(HEADS):
            cols = slice(h * DH, (h + 1) * DH)
            sel[kv * HEADS + h] = jnp.where(
                a_core == 0, buf[0, HALF:BLOCK, cols], buf[1, HALF:BLOCK, cols]
            )

    def s1_copy(j):
        return remote(sel.at[j], cand.at[lax.rem(xy, 8)], s1_s, s1_r, plane_dev(j))

    @pl.when(low_y)
    def _():
        @pl.loop(1, PLANE)
        def _(i):
            s1_copy(lax.rem(xy + i, PLANE)).start()

        cand[lax.rem(xy, 8)] = sel[xy]

    for i in range(2, 4):
        local_in[i].wait()
        remote_in[i].wait_recv()
    swap(0, EARLY, (False,))

    @pl.when(low_y)
    def _():
        landed(cand.at[pl.ds(0, 7)], s1_r)

    @pl.when(jnp.logical_not(low_y))
    def _():
        landed(cand, s1_r)

    zb[z] = cand[a_xy]

    def s2_copy(dz):
        return remote(zb.at[z], zb.at[z], s2_s, s2_r, z_dev(lax.rem(z + dz, 4)))

    for dz in range(1, 4):
        s2_copy(dz).start()
    landed(zb.at[pl.ds(0, 3)], s2_r)
    kva[xy, 0:HALF, :] = zb[a_zl]
    kva[xy, HALF:BLOCK, :] = zb[2 + a_zl]

    x, y = lax.rem(xy, 4), xy // 4

    def along(slot, k, on_x, step):
        dev = y * 4 + lax.rem(x + step, 4) if on_x else lax.rem(y + step, 4) * 4 + x
        part = kva.at[slot, pl.ds(k * HALF, HALF), :]
        return remote(part, part, s3_s, s3_r.at[slot, k], plane_dev(dev))

    def arrived(slot, k):
        landed(kva.at[slot, pl.ds(k * HALF, HALF), :], s3_r.at[slot, k])

    for second_leg in (False, True):
        for step in (1, 3, 2):
            for k in range(2):
                along(xy, k, (k == 0) != second_leg, step).start()

    swap(EARLY, AHEAD, (False,))
    swap(EARLY_OWN, AHEAD, (True,))

    for n in (1, 3, 2):
        for k in range(2):
            slot = y * 4 + lax.rem(x + n, 4) if k == 0 else lax.rem(y + n, 4) * 4 + x
            arrived(slot, k)
            for step in (1, 3, 2):
                along(slot, k, k == 1, step).start()

    block0 = seq - c
    row = lax.broadcasted_iota(jnp.int32, (HALF, BLOCK), 0)
    col = lax.broadcasted_iota(jnp.int32, (HALF, BLOCK), 1)
    own_ok = jnp.where(col < HALF, jnp.where(t == 1, 1, 0), jnp.where(row >= col - HALF, 1, 0)) > 0
    own_bias = jnp.where(own_ok, 0.0, LOW)
    own_bias = jnp.concatenate([own_bias, own_bias], 0)
    far_bias = jnp.concatenate(
        [
            jnp.where(col < jnp.where(block0 + p > a, offsets[block0 + p], 0), 0.0, LOW)
            for p in range(2)
        ],
        0,
    )

    def r1_copy(j):
        return remote(fk.at[j], rin.at[xy], r1_s, r1_r, plane_dev(j))

    def st_copy(b):
        return remote(st.at[b], sr.at[b], st_s.at[b], st_r.at[b], partner)

    lane = lax.broadcasted_iota(jnp.int32, (BLOCK, DH), 1)

    @pl.loop(0, HEADS)
    def _(i):
        h = lax.rem(xy + i, HEADS)
        cols = head_cols(h)

        @pl.when(i < HEADS - AHEAD)
        def _():
            swap(i + AHEAD, i + AHEAD + 1)

        for kv in range(2):
            slot = kv * HEADS + h

            @pl.when(slot != xy)
            def _():
                @pl.when(slot // 4 != y)
                def _():
                    arrived(slot, 0)

                @pl.when(lax.rem(slot, 4) != x)
                def _():
                    arrived(slot, 1)

        @pl.when(t == 1)
        def _():
            landed(cand.at[pl.ds(0, 4)], sw_r.at[h])

        q = [qb[p, :, cols] for p in range(2)]
        g = [gb[p, :, cols] for p in range(2)]
        keys = [kc[p, :, cols] for p in range(2)]
        values = [vc[p, :, cols] for p in range(2)]
        q2 = jnp.concatenate(q, 0)
        g2 = jnp.concatenate(g, 0)
        ka = kva[h]
        va = kva[HEADS + h]
        s_far = dot_t(q2, ka) * SCALE + far_bias
        s_own = jnp.concatenate([dot_t(q[p], keys[p]) for p in range(2)], 0) * SCALE + own_bias
        top = jnp.max(jnp.maximum(s_own, s_far), 1, keepdims=True)
        e_own = jnp.exp(s_own - top)
        e_far = jnp.exp(s_far - top)
        total = jnp.sum(e_own + e_far, 1, keepdims=True)
        inv = 1.0 / total
        w_own = e_own.astype(jnp.bfloat16)
        w_far = e_far.astype(jnp.bfloat16)
        w_half = [w_own[p * HALF : (p + 1) * HALF] for p in range(2)]
        mixed = dot(w_far, va) + jnp.concatenate([dot(w_half[p], values[p]) for p in range(2)], 0)
        mixed = mixed * inv
        scaled_g = (g2.astype(jnp.float32) * inv).astype(jnp.bfloat16)
        fk[HEADS + h] = t_dot(w_far, scaled_g).astype(jnp.bfloat16)

        @pl.when(HEADS + h != xy)
        def _():
            r1_copy(HEADS + h).start()

        att = mixed.astype(jnp.bfloat16)
        delta = jnp.sum(g2.astype(jnp.float32) * att.astype(jnp.float32), 1, keepdims=True)
        d_far = (e_far * ((dot_t(g2, va) - delta) * inv)).astype(jnp.bfloat16)
        dp_own = jnp.concatenate([dot_t(g[p], values[p]) for p in range(2)], 0)
        d_own = (e_own * ((dp_own - delta) * inv)).astype(jnp.bfloat16)
        d_half = [d_own[p * HALF : (p + 1) * HALF] for p in range(2)]
        fk[h] = (t_dot(d_far, q2) * SCALE).astype(jnp.bfloat16)
        @pl.when(h != xy)
        def _():
            r1_copy(h).start()

        batch = i // 4
        place = lax.rem(i, 4) * 4
        stats = st[batch]
        for k, value in enumerate((top, inv, delta)):
            stats = jnp.where(lane == place + k, value, stats)
        st[batch] = stats

        @pl.when(jnp.logical_and(t == 1, lax.rem(i, 4) == 3))
        def _():
            st_copy(batch).start()

        for p in range(2):
            okf[p, :, cols] = t_dot(d_half[p][:, HALF:], q[p]) * SCALE
            ovf[p, :, cols] = t_dot(w_half[p][:, HALF:], scaled_g[p * HALF : (p + 1) * HALF])

        grad_q = dot(d_far, ka) + jnp.concatenate([dot(d_half[p], keys[p]) for p in range(2)], 0)
        grad_q = (grad_q * SCALE).astype(jnp.bfloat16)
        for p in range(2):
            att_b[p, :, cols] = att[p * HALF : (p + 1) * HALF]
            gq_b[p, :, cols] = grad_q[p * HALF : (p + 1) * HALF]

    outs = ((att_b, att_out), (gq_b, gq_out), (gk_b, gk_out), (gv_b, gv_out))
    local_out = [
        pltpu.make_async_copy(buf.at[c], dst.at[:, mine], out_l.at[i]) for i, (buf, dst) in enumerate(outs)
    ]
    remote_out = [
        remote(buf.at[other], dst.at[:, mine], out_s.at[i], out_r.at[i], sibling)
        for i, (buf, dst) in enumerate(outs)
    ]
    for i in range(2):
        remote_out[i].start()
        local_out[i].start()

    def cross(begin, end):
        @pl.when(t == 0)
        def _():
            for b in range(begin // 4, (end + 3) // 4):
                if begin <= 4 * b:
                    st_copy(b).wait_recv()

            @pl.loop(begin, end)
            def _(i):
                h = lax.rem(xy + i, HEADS)
                cols = head_cols(h)
                landed(cand.at[pl.ds(0, 4)], sw_r.at[h])
                stats = sr[i // 4]
                place = lax.rem(i, 4) * 4
                top, inv, delta = [
                    jnp.sum(jnp.where(lane == place + k, stats, 0.0), 1, keepdims=True) for k in range(3)
                ]
                q = [q1b[p, :, cols] for p in range(2)]
                g = [g1b[p, :, cols] for p in range(2)]
                s = jnp.concatenate([dot_t(q[p], kc[p, HALF:BLOCK, cols]) for p in range(2)], 0) * SCALE
                dp = jnp.concatenate([dot_t(g[p], vc[p, HALF:BLOCK, cols]) for p in range(2)], 0)
                prob = jnp.exp(s - top) * inv
                w = prob.astype(jnp.bfloat16)
                d = (prob * (dp - delta)).astype(jnp.bfloat16)
                for p in range(2):
                    rows = slice(p * HALF, (p + 1) * HALF)
                    okf[p, :, cols] += t_dot(d[rows], q[p]) * SCALE
                    ovf[p, :, cols] += t_dot(w[rows], g[p])

    for copy in remote_in:
        copy.wait_send()

    @pl.when(low_y)
    def _():
        sent(sel.at[pl.ds(0, PLANE - 1)], s1_s)

    sent(zb.at[pl.ds(0, 3)], s2_s)
    sent(kva.at[pl.ds(0, PLANE - 1)], s3_s)
    sent(kc, sw_s)

    landed(rin.at[pl.ds(0, PLANE - 1)], r1_r)
    rin[xy] = fk[xy]
    acc = rin[0].astype(jnp.float32)
    for slot in range(1, PLANE):
        acc = acc + rin[slot].astype(jnp.float32)
    zs[0] = acc[:HALF].astype(jnp.bfloat16)
    zs[1] = acc[HALF:].astype(jnp.bfloat16)

    def r2_copy(dz):
        z_ = lax.rem(z + dz, 4)
        return remote(zs.at[z_ // 2], zr.at[z], r2_s, r2_r, z_dev(z_))

    for dz in range(1, 4):
        r2_copy(dz).start()
    zr[z] = zs[t]
    cross(0, 4)
    sent(fk.at[pl.ds(0, PLANE - 1)], r1_s)
    landed(zr.at[pl.ds(0, 3)], r2_r)
    total = zr[0].astype(jnp.float32)
    for slot in range(1, 4):
        total = total + zr[slot].astype(jnp.float32)
    an[...] = total.astype(jnp.bfloat16)

    def r3_copy(j):
        return remote(an, ank.at[xy], r3_s, r3_r, plane_dev(j))

    @pl.loop(0, 8)
    def _(i):
        j = lax.rem(xy + i, 8)

        @pl.when(j != xy)
        def _():
            r3_copy(j).start()

    cross(4, HEADS)
    sent(zr.at[pl.ds(0, 3)], r2_s)

    @pl.when(t == 1)
    def _():
        for b in range(2):
            st_copy(b).wait_send()

    @pl.when(low_y)
    def _():
        ank[xy] = an[...]
        landed(ank.at[pl.ds(0, PLANE - 1)], r3_r)

    for p in (other, c):
        for kv, (grads, out) in enumerate(((okf, gk_b), (ovf, gv_b))):
            owner = block0 + p == a

            @pl.when(low_y)
            def _():
                for h in range(HEADS):
                    cols = slice(h * DH, (h + 1) * DH)
                    far = jnp.where(owner, ank[kv * HEADS + h].astype(jnp.float32), 0.0)
                    out[p, :, cols] = (grads[p, :, cols] + far).astype(jnp.bfloat16)

            @pl.when(jnp.logical_not(low_y))
            def _():
                out[p] = grads[p].astype(jnp.bfloat16)

            if p is other:
                remote_out[2 + kv].start()
            else:
                local_out[2 + kv].start()

    @pl.when(low_y)
    def _():
        sent(ank.at[pl.ds(0, 7)], r3_s)

    @pl.when(jnp.logical_not(low_y))
    def _():
        sent(ank.at[pl.ds(0, 8)], r3_s)

    for copy in local_out:
        copy.wait()
    for copy in remote_out:
        copy.wait()


def write_out(*refs):
    sems, sems2, hold = refs[8:]
    first = [pltpu.make_async_copy(refs[i], hold.at[i], sems.at[i]) for i in range(4)]
    second = [pltpu.make_async_copy(hold.at[i], refs[4 + i], sems2.at[i]) for i in range(4)]
    for copy in first:
        copy.start()
    for i in range(4):
        first[i].wait()
        second[i].start()
    for copy in second:
        copy.wait()


def on_device(queries, key_rows, value_rows, grad_out, anchor, offsets):
    bf16, f32 = jnp.bfloat16, jnp.float32
    any_spec = pl.BlockSpec(memory_space=pl.ANY)
    smem_spec = pl.BlockSpec(memory_space=pltpu.SMEM)
    dma = pltpu.SemaphoreType.DMA
    half = (HALF, DH)
    whole = (BLOCK, DH)
    scratch = [
        pltpu.VMEM((2, HALF, WIDE), bf16),
        pltpu.VMEM((2, HALF, WIDE), bf16),
        pltpu.VMEM((2, BLOCK, WIDE), bf16),
        pltpu.VMEM((2, BLOCK, WIDE), bf16),
        pltpu.VMEM((PLANE, *half), bf16),
        pltpu.VMEM((8, *half), bf16),
        pltpu.VMEM((4, *half), bf16),
        pltpu.VMEM((PLANE, *whole), bf16),
        pltpu.VMEM((PLANE, *whole), bf16),
        pltpu.VMEM((PLANE, *whole), bf16),
        pltpu.VMEM((2, *half), bf16),
        pltpu.VMEM((4, *half), bf16),
        pltpu.VMEM(half, bf16),
        pltpu.VMEM((PLANE, *half), bf16),
        pltpu.VMEM((2, HALF, WIDE), f32),
        pltpu.VMEM((2, HALF, WIDE), f32),
        pltpu.VMEM((2, HALF, WIDE), bf16),
        pltpu.VMEM((2, HALF, WIDE), bf16),
        pltpu.VMEM((2, BLOCK, DH), f32),
        pltpu.VMEM((2, BLOCK, DH), f32),
        pltpu.VMEM((2, HALF, WIDE), bf16),
        pltpu.VMEM((2, HALF, WIDE), bf16),
        pltpu.VMEM((2, HALF, WIDE), bf16),
        pltpu.VMEM((2, HALF, WIDE), bf16),
        dma((4,)), dma((4,)), dma((4,)),
        dma, dma((HEADS,)),
        dma, dma,
        dma, dma,
        dma, dma((PLANE, 2)),
        dma, dma,
        dma, dma,
        dma, dma,
        dma((2,)), dma((2,)),
        dma((4,)), dma((4,)), dma((4,)),
    ]
    results = pl.pallas_call(
        kernel,
        out_shape=[jax.ShapeDtypeStruct(queries.shape, bf16)] * 4,
        in_specs=[smem_spec, smem_spec] + [pl.BlockSpec(memory_space=pltpu.HBM)] * 4,
        out_specs=[any_spec] * 4,
        scratch_shapes=scratch,
        compiler_params=pltpu.CompilerParams(
            collective_id=0, has_side_effects=True, vmem_limit_bytes=60 * 2**20
        ),
        name="anchor_attention",
    )(anchor, offsets, queries, key_rows, value_rows, grad_out)
    return pl.pallas_call(
        write_out,
        out_shape=[jax.ShapeDtypeStruct(queries.shape, bf16)] * 4,
        in_specs=[any_spec] * 4,
        out_specs=[pl.BlockSpec(memory_space=pltpu.HBM)] * 4,
        scratch_shapes=[dma((4,)), dma((4,)), pltpu.VMEM((4, *queries.shape), bf16)],
        name="write_out",
    )(*results)


def solution(mesh):
    tokens = P(("seq", "head"), None)
    return jax.shard_map(
        on_device,
        mesh=mesh,
        in_specs=(tokens, tokens, tokens, tokens, P(), P()),
        out_specs=(tokens, tokens, tokens, tokens),
        check_vma=False,
    )
```
